32 devices in a mesh: section: 16 (over z, y, x), dp: 2 (over core).
Axes of the slice: x: 2, y: 2, z: 4, core: 2. Of those that a mesh axis runs over, the one named last changes fastest.
Arguments:
- act_down: bfloat16 [16, 2, 512, 1024], P('section', None, 'dp'), may hold values from -6 to 6
- act_up: bfloat16 [16, 2, 512, 1024], P('section', None, 'dp'), may hold values from -6 to 6
- grad_down: bfloat16 [16, 512, 1024], P('section', 'dp'), may hold values from -1.5 to 1.5
- grad_up: bfloat16 [16, 512, 1024], P('section', 'dp'), may hold values from -1.5 to 1.5
- seed_down: bfloat16 [512, 1024], P('dp'), may hold values from -1.5 to 1.5
- seed_up: bfloat16 [512, 1024], P('dp'), may hold values from -1.5 to 1.5
- gain_down: float32 [16, 1024], P('section'), as said below
- qkv_down: bfloat16 [16, 1024, 768], P('section'), as said below
- outproj_down: bfloat16 [16, 512, 1024], P('section'), as said below
- gain_up: float32 [16, 1024], P('section'), as said below
- qkv_up: bfloat16 [16, 1024, 768], P('section'), as said below
- outproj_up: bfloat16 [16, 512, 1024], P('section'), as said below
- doc_offsets: int32 [2, 16, 2, 2], P(None, 'section', None, 'dp'), may hold values from 1 to 255
- slot_order: int32 [2, 16, 2], P(None, 'section'), may hold values from 0 to 1, each once within a row
Outputs:
- input_grads: bfloat16 [2, 16, 2, 512, 1024], P(None, 'section', None, 'dp')
- grad_gain: float32 [16, 1024], P('section', 'dp')
- grad_qkv: float32 [16, 1024, 768], P('section', 'dp')
- grad_outproj: float32 [16, 512, 1024], P('section', 'dp')
The draws below stay inside these ranges and needn't reach their ends.
Inputs may be any that keep to these rules, and one draw needn't show every extreme that they name: `gain_down`: the down copy of every layer. `qkv_down`: the down copy of every layer. `outproj_down`: the down copy of every layer. gain_up[s] equals gain_down[15 - s]. qkv_up[s] equals qkv_down[15 - s]. outproj_up[s] equals outproj_down[15 - s]. `doc_offsets`: each sequence holds two documents; the value is the position where the second begins. `slot_order`: each row of a direction and section names 0 and 1 once each.
All inputs are finite; a program needn't handle non-finite values.
Results may differ from the reference program's by a relative error of at most 0.015.
Values may be sent and summed in bfloat16 or wider, within the bound.
No kernel may reach another device: no remote copies, remote signals or barrier semaphores. Data moves between devices by JAX's collectives and lax.ppermute only.
A program may use at most 128 MiB of HBM per device.

```python
import math
import jax
import jax.numpy as jnp
from jax import lax

D = 1024
HEADS = 8
KV_HEADS = 2
SEQ = 256
QW = 512
QKV = 768
LAYERS = 16
REPLICAS = 2
TOKENS = 512


def mirrored_layers(key):
    base = jax.random.fold_in(key, 31)
    key_gain = jax.random.fold_in(base, 1)
    key_qkv = jax.random.fold_in(base, 2)
    key_out = jax.random.fold_in(base, 3)
    gains = jax.random.uniform(key_gain, (LAYERS, D), jnp.float32, 0.6, 1.4)
    qkv = jax.random.normal(key_qkv, (LAYERS, D, QKV), jnp.float32) / math.sqrt(D)
    outproj = jax.random.normal(key_out, (LAYERS, QW, D), jnp.float32) / math.sqrt(QW)
    return (gains, qkv.astype(jnp.bfloat16), outproj.astype(jnp.bfloat16))


def draw_gain_down(key, part):
    return mirrored_layers(key)[0]


def draw_qkv_down(key, part):
    return mirrored_layers(key)[1]


def draw_outproj_down(key, part):
    return mirrored_layers(key)[2]


def draw_gain_up(key, part):
    return jnp.flip(mirrored_layers(key)[0], axis=0)


def draw_qkv_up(key, part):
    return jnp.flip(mirrored_layers(key)[1], axis=0)


def draw_outproj_up(key, part):
    return jnp.flip(mirrored_layers(key)[2], axis=0)


def place_ends(drawn, key, smallest, top_value):
    longest = drawn.shape.index(max(drawn.shape))
    spots = []
    for shift in (0, 1):
        where = [jax.random.randint(jax.random.fold_in(key, axis), (), 0, length) for axis, length in enumerate(drawn.shape)]
        where[longest] = (where[longest] + shift) % drawn.shape[longest]
        spots.append(tuple(where))
    return drawn.at[spots[0]].set(smallest).at[spots[1]].set(top_value)


def block_levels(rng, shape, shards, low, top_value):
    gain, own = 1.0, jax.random.fold_in(rng, 6)
    for dim, shards_of in shards:
        steps = jnp.exp(jax.random.uniform(jax.random.fold_in(own, dim), (shards_of,), jnp.float32, low / len(shards), top_value / len(shards)))
        gain = gain * jnp.repeat(steps, shape[dim] // shards_of).reshape([-1 if axis == dim else 1 for axis in range(len(shape))])
    return gain


def centred(own_key, shape, spread, limit, shards=(), kind=jnp.bfloat16):
    factor_of = block_levels(own_key, shape, shards, -0.22, 0.18) if shards else 1.0
    result = jax.random.normal(own_key, shape, jnp.float32) * spread * factor_of
    return jnp.minimum(jnp.maximum(result, -limit), limit).astype(kind)


def setup_inputs(seed: int = 0) -> dict:
    streams_of = jax.random.split(jax.random.key(seed), 15)
    return {
        "act_down": centred(streams_of[0], (LAYERS, 2, TOKENS, D), 1.0, 6.0, ((0, 16), (2, 2))),
        "act_up": centred(streams_of[1], (LAYERS, 2, TOKENS, D), 1.0, 6.0, ((0, 16), (2, 2))),
        "grad_down": centred(streams_of[2], (LAYERS, TOKENS, D), 0.25, 1.5, ((0, 16), (1, 2))),
        "grad_up": centred(streams_of[3], (LAYERS, TOKENS, D), 0.25, 1.5, ((0, 16), (1, 2))),
        "seed_down": centred(streams_of[4], (TOKENS, D), 0.25, 1.5, ((0, 2),)),
        "seed_up": centred(streams_of[5], (TOKENS, D), 0.25, 1.5, ((0, 2),)),
        "gain_down": draw_gain_down(jax.random.fold_in(streams_of[14], 71), 0),
        "qkv_down": draw_qkv_down(jax.random.fold_in(streams_of[14], 71), 0),
        "outproj_down": draw_outproj_down(jax.random.fold_in(streams_of[14], 71), 0),
        "gain_up": draw_gain_up(jax.random.fold_in(streams_of[14], 71), 0),
        "qkv_up": draw_qkv_up(jax.random.fold_in(streams_of[14], 71), 0),
        "outproj_up": draw_outproj_up(jax.random.fold_in(streams_of[14], 71), 0),
        "doc_offsets": place_ends(jax.random.randint(streams_of[12], (2, LAYERS, 2, REPLICAS), 1, SEQ), jax.random.fold_in(streams_of[12], 1), 1, SEQ - 1).astype(jnp.int32),
        "slot_order": jax.vmap(lambda own: jax.random.permutation(own, 2))(jax.random.split(streams_of[13], 2 * LAYERS)).reshape((2, LAYERS, 2)).astype(jnp.int32),
    }


EPSILON = 1e-05

def backward_layer(inputs, gain_vec, qkv_weight, out_weight, offset, upstream):
    seq_len = inputs.shape[0]
    query_width = out_weight.shape[0]
    pair_width = (qkv_weight.shape[1] - query_width) // 2
    group_size = HEADS // KV_HEADS
    head_width = query_width // HEADS
    score_scale = head_width ** (-0.5)
    xfloat = inputs.astype(jnp.float32)
    inverse = lax.rsqrt(lax.optimization_barrier(jnp.mean(xfloat * xfloat, axis=1, keepdims=True)) + EPSILON)
    scaled = xfloat * inverse
    normed = (scaled * gain_vec).astype(jnp.bfloat16)
    project = jnp.dot(normed, qkv_weight, preferred_element_type=jnp.float32).astype(jnp.bfloat16)
    queries = project[:, :query_width].reshape(seq_len, KV_HEADS, group_size, head_width).astype(jnp.float32)
    keys_all = project[:, query_width:query_width + pair_width].reshape(seq_len, KV_HEADS, head_width).astype(jnp.float32)
    values = project[:, query_width + pair_width:].reshape(seq_len, KV_HEADS, head_width).astype(jnp.float32)
    positions = jnp.arange(seq_len, dtype=jnp.int32)
    second_doc = positions >= offset
    allowed = (positions[None, :] <= positions[:, None]) & (second_doc[None, :] == second_doc[:, None])
    scores = jnp.einsum('igha,jga->ghij', queries, keys_all) * score_scale
    scores = jnp.where(allowed, scores, -1e+30)
    row_top = lax.optimization_barrier(jnp.max(scores, axis=3, keepdims=True))
    raised = jnp.exp(scores - row_top)
    soft_weights = raised / lax.optimization_barrier(jnp.sum(raised, axis=3, keepdims=True))
    soft_low = soft_weights.astype(jnp.bfloat16)
    soft_wide = soft_low.astype(jnp.float32)
    attended = jnp.einsum('ghij,jga->igha', soft_wide, values).reshape(seq_len, query_width).astype(jnp.bfloat16)
    grad_out = jnp.dot(attended.T, upstream, preferred_element_type=jnp.float32)
    grad_attended = jnp.dot(upstream, out_weight.T, preferred_element_type=jnp.float32).astype(jnp.bfloat16)
    grad_heads = grad_attended.reshape(seq_len, KV_HEADS, group_size, head_width).astype(jnp.float32)
    grad_values = jnp.einsum('ghij,igha->jga', soft_wide, grad_heads)
    grad_soft = jnp.einsum('igha,jga->ghij', grad_heads, values)
    grad_scores = (soft_weights * (grad_soft - lax.optimization_barrier(jnp.sum(soft_weights * grad_soft, axis=3, keepdims=True))) * score_scale).astype(jnp.bfloat16)
    scores_wide = grad_scores.astype(jnp.float32)
    grad_queries = jnp.einsum('ghij,jga->igha', scores_wide, keys_all)
    grad_keys = jnp.einsum('ghij,igha->jga', scores_wide, queries)
    grad_project = jnp.concatenate([grad_queries.reshape(seq_len, query_width), grad_keys.reshape(seq_len, pair_width), grad_values.reshape(seq_len, pair_width)], axis=1).astype(jnp.bfloat16)
    grad_qkv = jnp.dot(normed.T, grad_project, preferred_element_type=jnp.float32)
    grad_normed = jnp.dot(grad_project, qkv_weight.T, preferred_element_type=jnp.float32)
    grad_gain = lax.optimization_barrier(jnp.sum(grad_normed * scaled, axis=0))
    grad_hat = grad_normed * gain_vec
    grad_inputs = upstream.astype(jnp.float32) + inverse * (grad_hat - scaled * lax.optimization_barrier(jnp.mean(grad_hat * scaled, axis=1, keepdims=True)))
    return (grad_inputs.astype(jnp.bfloat16), grad_gain, grad_qkv, grad_out)

def rounded_sum(term):
    low = lax.optimization_barrier(term.astype(jnp.bfloat16))
    return lax.optimization_barrier(jnp.sum(low.astype(jnp.float32), axis=0))

def run_direction(acts, first_grads, seeds, gains, qkv_weights, out_weights, offsets, order_rows, from_top):
    first_zero = order_rows[:, 0] == 0
    second_zero = order_rows[:, 1] == 0
    acts_one = jnp.where(first_zero[:, None, None], acts[:, 0], acts[:, 1]).reshape(LAYERS, REPLICAS, SEQ, D)
    acts_two = jnp.where(second_zero[:, None, None], acts[:, 0], acts[:, 1]).reshape(LAYERS, REPLICAS, SEQ, D)
    offs_one = jnp.where(first_zero[:, None], offsets[:, 0], offsets[:, 1])
    offs_two = jnp.where(second_zero[:, None], offsets[:, 0], offsets[:, 1])
    upstream_one = first_grads.reshape(LAYERS, REPLICAS, SEQ, D)
    batched = jax.vmap(backward_layer, in_axes=(0, None, None, None, 0, 0))

    def section_step(carry, items):
        acts_a, acts_b, upstream_a, gain_vec, qkv_weight, out_weight, offs_a, offs_b = items
        one = batched(acts_a, gain_vec, qkv_weight, out_weight, offs_a, upstream_a)
        two = batched(acts_b, gain_vec, qkv_weight, out_weight, offs_b, carry)
        gain_sum = rounded_sum(one[1] + two[1])
        qkv_sum = rounded_sum(one[2] + two[2])
        out_sum = rounded_sum(one[3] + two[3])
        return (one[0], (one[0], two[0], gain_sum, qkv_sum, out_sum))
    items = (acts_one, acts_two, upstream_one, gains, qkv_weights, out_weights, offs_one, offs_two)
    seeds_split = seeds.reshape(REPLICAS, SEQ, D)
    unused, stacked = lax.scan(section_step, seeds_split, items, reverse=from_top)
    grads_one, grads_two, gain_sums, qkv_sums, out_sums = stacked
    input_grads = jnp.stack([grads_one, grads_two], axis=1).reshape(LAYERS, 2, TOKENS, D)
    return (input_grads, gain_sums, qkv_sums, out_sums)

def reference(act_down, act_up, grad_down, grad_up, seed_down, seed_up, gain_down, qkv_down, outproj_down, gain_up, qkv_up, outproj_up, doc_offsets, slot_order):
    down = run_direction(act_down, grad_down, seed_down, gain_down, qkv_down, outproj_down, doc_offsets[0], slot_order[0], True)
    upper = run_direction(act_up, grad_up, seed_up, gain_up, qkv_up, outproj_up, doc_offsets[1], slot_order[1], False)
    input_grads = jnp.stack([down[0], upper[0]], axis=0)
    grad_gain = down[1] + jnp.flip(upper[1], axis=0)
    grad_qkv = down[2] + jnp.flip(upper[2], axis=0)
    grad_outproj = down[3] + jnp.flip(upper[3], axis=0)
    return (input_grads, grad_gain, grad_qkv, grad_outproj)
```

```python
import functools
import jax
import jax.numpy as jnp
from jax import lax
from jax.experimental import pallas as pl
from jax.experimental.pallas import tpu as pltpu
from jax.sharding import PartitionSpec as P

HEADS = 8
KV_HEADS = 2
EPSILON = 1e-05
MASKED = -1e30
PAD = 16
VMEM_LIMIT = 32 * 1024 * 1024
F32 = jnp.float32
BF16 = jnp.bfloat16
NN = (((1,), (0,)), ((), ()))
NT = (((1,), (1,)), ((), ()))
TN = (((0,), (0,)), ((), ()))


def dot(a, b, dims=NN):
    return lax.dot_general(a, b, dims, preferred_element_type=F32)


def doubled(pair, half):
    wide = pair.astype(F32)
    turned = pltpu.roll(wide, half, 1)
    left = lax.broadcasted_iota(jnp.int32, wide.shape, 1) < half
    zero = jnp.zeros_like(wide)
    out = []
    for g in range(KV_HEADS):
        a, b = (wide, turned) if g == 0 else (turned, wide)
        out.append(
            jnp.concatenate([jnp.where(left, a, zero), jnp.where(left, zero, b)], axis=0).astype(BF16)
        )
    return out


def mask_bias(seq, offset):
    row = lax.broadcasted_iota(jnp.int32, (seq, seq), 0)
    col = lax.broadcasted_iota(jnp.int32, (seq, seq), 1)
    start = jnp.where(row >= offset, offset, 0)
    return jnp.where((col <= row) & (col >= start), 0.0, MASKED).astype(F32)


def normalise(x, gain):
    xf = x.astype(F32)
    inverse = lax.rsqrt(jnp.mean(xf * xf, axis=1, keepdims=True) + EPSILON)
    scaled = xf * inverse
    return inverse, scaled, (scaled * gain).astype(BF16)


def forward_heads(project, offset, query_width, soft_ref):
    seq = project.shape[0]
    half = query_width // HEADS
    wide = 2 * half
    keys = doubled(project[:, query_width : query_width + wide], half)
    values = doubled(project[:, query_width + wide :], half)
    bias = mask_bias(seq, offset)
    scale = half ** (-0.5)
    pairs = HEADS // 2
    attended = []
    for p in range(pairs):
        g = p * KV_HEADS // pairs
        queries = project[:, p * wide : (p + 1) * wide] * jnp.asarray(scale, BF16)
        scores = dot(queries, keys[g], NT)
        for t in range(2):
            s = scores[:, t * seq : (t + 1) * seq] + bias
            e = jnp.exp(s - jnp.max(s, axis=1, keepdims=True))
            soft = e * (1.0 / jnp.sum(e, axis=1, keepdims=True))
            soft_ref[p, :, t * seq : (t + 1) * seq] = soft.astype(BF16)
        attended.append(dot(soft_ref[p], values[g]))
    return attended


def backward_heads(project, attended, grad_attended, query_width, soft_ref):
    seq = project.shape[0]
    half = query_width // HEADS
    wide = 2 * half
    keys = doubled(project[:, query_width : query_width + wide], half)
    values = doubled(project[:, query_width + wide :], half)
    scale = half ** (-0.5)
    pairs = HEADS // 2
    left = lax.broadcasted_iota(jnp.int32, (seq, wide), 1) < half
    grad_queries = []
    grad_keys = [None] * KV_HEADS
    grad_values = [None] * KV_HEADS
    for p in range(pairs):
        g = p * KV_HEADS // pairs
        queries = project[:, p * wide : (p + 1) * wide] * jnp.asarray(scale, BF16)
        grad_pair = grad_attended[:, p * wide : (p + 1) * wide]
        grad_soft = dot(grad_pair, values[g], NT)
        both = attended[p].astype(F32) * grad_pair.astype(F32)
        rows = [
            jnp.sum(jnp.where(left, both, 0.0), axis=1, keepdims=True),
            jnp.sum(jnp.where(left, 0.0, both), axis=1, keepdims=True),
        ]
        soft = soft_ref[p]
        grad_scores = jnp.concatenate(
            [
                (
                    soft[:, t * seq : (t + 1) * seq].astype(F32)
                    * (grad_soft[:, t * seq : (t + 1) * seq] - rows[t])
                ).astype(BF16)
                for t in range(2)
            ],
            axis=1,
        )
        grad_queries.append(dot(grad_scores, keys[g]) * scale)
        keys_part = dot(queries, grad_scores, TN)
        values_part = dot(grad_pair, soft, TN)
        keys_sum = keys_part[:half, :seq] + keys_part[half:, seq:]
        values_sum = values_part[:half, :seq] + values_part[half:, seq:]
        grad_keys[g] = keys_sum if grad_keys[g] is None else grad_keys[g] + keys_sum
        grad_values[g] = values_sum if grad_values[g] is None else grad_values[g] + values_sum
    columns = grad_queries + [
        jnp.concatenate(grad_keys, axis=0).T,
        jnp.concatenate(grad_values, axis=0).T,
    ]
    return jnp.concatenate([c.astype(BF16) for c in columns], axis=1)


def input_gradient(grad_project, qkv, gain, scaled, inverse, upstream):
    grad_normed = dot(grad_project, qkv, NT)
    grad_hat = grad_normed * gain
    part = grad_normed * scaled
    grad_gain = jnp.sum(part, axis=0, keepdims=True)
    mean = jnp.mean(part * gain, axis=1, keepdims=True)
    grad_in = upstream.astype(F32) + inverse * (grad_hat - scaled * mean)
    return grad_in.astype(BF16), grad_gain


def first_kernel(
    scalars, act, qkv_hbm, out_hbm, up_hbm, gain_ref,
    grad_ref, normed_ref, attended_ref, project_ref, gain_out,
    x_ref, qkv_ref, out_ref, up_ref, soft_ref, sems,
):
    copies = [
        pltpu.make_async_copy(act.at[scalars[0]], x_ref, sems.at[0]),
        pltpu.make_async_copy(qkv_hbm, qkv_ref, sems.at[1]),
        pltpu.make_async_copy(up_hbm, up_ref, sems.at[2]),
        pltpu.make_async_copy(out_hbm, out_ref, sems.at[3]),
    ]
    for copy in copies:
        copy.start()
    query_width = out_hbm.shape[0]
    gain = gain_ref[...]
    copies[0].wait()
    inverse, scaled, normed = normalise(x_ref[...], gain)
    normed_ref[...] = normed
    copies[1].wait()
    project = dot(normed, qkv_ref[...]).astype(BF16)
    attended = forward_heads(project, scalars[1], query_width, soft_ref)
    attended_ref[...] = jnp.concatenate([a.astype(BF16) for a in attended], axis=1)
    copies[2].wait()
    copies[3].wait()
    grad_attended = dot(up_ref[...], out_ref[...], NT).astype(BF16)
    grad_project = backward_heads(project, attended, grad_attended, query_width, soft_ref)
    project_ref[...] = grad_project
    inverse, scaled, _ = normalise(x_ref[...], gain)
    grad_ref[...], gain_out[...] = input_gradient(
        grad_project, qkv_ref[...], gain, scaled, inverse, up_ref[...]
    )


def whole(memory=pltpu.VMEM):
    return pl.BlockSpec(memory_space=memory)


def first_pass(scalars, act, gain, qkv, out, upstream):
    seq, model = act.shape[1:]
    width = qkv.shape[1]
    query_width = out.shape[0]
    shape = jax.ShapeDtypeStruct
    return pl.pallas_call(
        first_kernel,
        out_shape=(
            shape((seq, model), BF16),
            shape((seq, model), BF16),
            shape((seq, query_width), BF16),
            shape((seq, width), BF16),
            shape((1, model), F32),
        ),
        in_specs=[whole(pltpu.SMEM)] + [whole(pl.ANY)] * 4 + [whole()],
        out_specs=[whole()] * 5,
        scratch_shapes=[
            pltpu.VMEM((seq, model), BF16),
            pltpu.VMEM((model, width), BF16),
            pltpu.VMEM((query_width, model), BF16),
            pltpu.VMEM((seq, model), BF16),
            pltpu.VMEM((HEADS // 2, seq, 2 * seq), BF16),
            pltpu.SemaphoreType.DMA((4,)),
        ],
        compiler_params=pltpu.CompilerParams(vmem_limit_bytes=VMEM_LIMIT),
        cost_estimate=pl.CostEstimate(flops=2 * 10**9, bytes_accessed=6 * 10**6, transcendentals=HEADS * seq * seq),
        name="first_pass",
    )(scalars, act, qkv, out, upstream, gain)


def forward_kernel(
    scalars, act, qkv_hbm, gain_ref, normed_ref, project_ref, attended_ref, soft_ref, x_ref, qkv_ref, sems, *, query_width
):
    copies = [
        pltpu.make_async_copy(act.at[scalars[0]], x_ref, sems.at[0]),
        pltpu.make_async_copy(qkv_hbm, qkv_ref, sems.at[1]),
    ]
    for copy in copies:
        copy.start()
    copies[0].wait()
    _, _, normed = normalise(x_ref[...], gain_ref[...])
    normed_ref[...] = normed
    copies[1].wait()
    project = dot(normed, qkv_ref[...]).astype(BF16)
    project_ref[...] = project
    attended = forward_heads(project, scalars[1], query_width, soft_ref)
    attended_ref[...] = jnp.concatenate([a.astype(BF16) for a in attended], axis=1)


def forward_pass(scalars, act, gain, qkv, query_width):
    seq, model = act.shape[1:]
    width = qkv.shape[1]
    shape = jax.ShapeDtypeStruct
    return pl.pallas_call(
        functools.partial(forward_kernel, query_width=query_width),
        out_shape=(
            shape((seq, model), BF16),
            shape((seq, width), BF16),
            shape((seq, query_width), BF16),
            shape((HEADS // 2, seq, 2 * seq), BF16),
        ),
        in_specs=[whole(pltpu.SMEM)] + [whole(pl.ANY)] * 2 + [whole()],
        out_specs=[whole()] * 4,
        scratch_shapes=[
            pltpu.VMEM((seq, model), BF16),
            pltpu.VMEM((model, width), BF16),
            pltpu.SemaphoreType.DMA((2,)),
        ],
        compiler_params=pltpu.CompilerParams(vmem_limit_bytes=VMEM_LIMIT),
        cost_estimate=pl.CostEstimate(flops=10**9, bytes_accessed=4 * 10**6, transcendentals=HEADS * seq * seq),
        name="forward_pass",
    )(scalars, act, qkv, gain)


def hand_out(blocks, scalars, send_ref, keep_ref):
    parts = blocks.shape[0]
    replica = scalars[3]
    for k in range(parts - 1):
        send_ref[k] = blocks[lax.rem(replica + 1 + k, parts)]
    keep_ref[...] = blocks[replica]


def outproj_kernel(scalars, att1, att2, up1, moved, seed, send_ref, keep_ref, up_ref, blocks):
    seeded = scalars[2] == 1

    @pl.when(seeded)
    def _():
        up_ref[...] = seed[...]

    @pl.when(jnp.logical_not(seeded))
    def _():
        up_ref[...] = moved[...]

    parts, rows, model = blocks.shape
    total = dot(att1[...], up1[...], TN) + dot(att2[...], up_ref[...], TN)
    for q in range(parts):
        blocks[q] = total[q * rows : (q + 1) * rows].astype(BF16)
    hand_out(blocks, scalars, send_ref, keep_ref)


def outproj_pass(scalars, att1, att2, up1, moved, seed, parts):
    seq, model = up1.shape
    rows = att1.shape[1] // parts
    shape = jax.ShapeDtypeStruct
    return pl.pallas_call(
        outproj_kernel,
        out_shape=(shape((parts - 1, rows, model), BF16), shape((rows, model), BF16), shape((seq, model), BF16)),
        in_specs=[whole(pltpu.SMEM)] + [whole()] * 5,
        out_specs=[whole()] * 3,
        scratch_shapes=[pltpu.VMEM((parts, rows, model), BF16)],
        compiler_params=pltpu.CompilerParams(vmem_limit_bytes=VMEM_LIMIT),
        cost_estimate=pl.CostEstimate(flops=10**9, bytes_accessed=4 * 10**6, transcendentals=0),
        name="outproj_pass",
    )(scalars, att1, att2, up1, moved, seed)


def second_kernel(
    scalars, act, project_ref, attended_ref, soft_ref, normed2, normed1, gproj1, gain1, up_ref, qkv_ref, out_ref, gain_ref,
    grad_ref, send_ref, keep_ref,
    x_ref, gproj2, blocks, sem,
):
    copy = pltpu.make_async_copy(act.at[scalars[0]], x_ref, sem)
    copy.start()
    query_width = out_ref.shape[0]
    wide = 2 * query_width // HEADS
    gain = gain_ref[...]
    grad_attended = dot(up_ref[...], out_ref[...], NT).astype(BF16)
    attended = [attended_ref[:, p * wide : (p + 1) * wide] for p in range(HEADS // 2)]
    gproj2[...] = backward_heads(project_ref[...], attended, grad_attended, query_width, soft_ref)
    copy.wait()
    inverse, scaled, _ = normalise(x_ref[...], gain)
    grad_ref[...], grad_gain = input_gradient(gproj2[...], qkv_ref[...], gain, scaled, inverse, up_ref[...])
    grad_gain = grad_gain + gain1[...]
    parts, height, width = blocks.shape
    rows = normed1.shape[1] // parts
    pad = height - rows
    for q in range(parts):
        at = slice(q * rows, (q + 1) * rows)
        total = dot(normed1[:, at], gproj1[...], TN) + dot(normed2[:, at], gproj2[...], TN)
        blocks[q, :rows, :] = total.astype(BF16)
        blocks[q, rows:, :] = jnp.zeros((pad, width), BF16)
        blocks[q, rows:, :rows] = jnp.broadcast_to(grad_gain[:, at], (pad, rows)).astype(BF16)
    hand_out(blocks, scalars, send_ref, keep_ref)


def second_pass(scalars, act, forward, first, upstream, gain, qkv, out, parts):
    seq, model = act.shape[1:]
    width = qkv.shape[1]
    height = model // parts + PAD
    normed2, project2, attended2, soft2 = forward
    shape = jax.ShapeDtypeStruct
    return pl.pallas_call(
        second_kernel,
        out_shape=(
            shape((seq, model), BF16),
            shape((parts - 1, height, width), BF16),
            shape((height, width), BF16),
        ),
        in_specs=[whole(pltpu.SMEM), whole(pl.ANY)] + [whole()] * 11,
        out_specs=[whole()] * 3,
        scratch_shapes=[
            pltpu.VMEM((seq, model), BF16),
            pltpu.VMEM((seq, width), BF16),
            pltpu.VMEM((parts, height, width), BF16),
            pltpu.SemaphoreType.DMA(()),
        ],
        compiler_params=pltpu.CompilerParams(vmem_limit_bytes=VMEM_LIMIT),
        cost_estimate=pl.CostEstimate(flops=2 * 10**9, bytes_accessed=6 * 10**6, transcendentals=0),
        name="second_pass",
    )(scalars, act, project2, attended2, soft2, normed2, first[1], first[3], first[4], upstream, qkv, out, gain)


def shifted(value, axis, steps):
    count = lax.axis_size(axis)
    first, last = (max(0, -steps), min(count, count - steps))
    return lax.ppermute(value, axis, [(source, source + steps) for source in range(first, last)])


def mirrored(value, axis):
    count = lax.axis_size(axis)
    return lax.ppermute(value, axis, [(i, count - 1 - i) for i in range(count)])


def replica_sum(send, keep, axis):
    parts = lax.axis_size(axis)
    total = keep.astype(F32)
    for k in range(parts - 1):
        moved = lax.ppermute(send[k], axis, [(i, (i + 1 + k) % parts) for i in range(parts)])
        total = total + moved.astype(F32)
    return total


def shards(
    act_down, act_up, grad_down, grad_up, seed_down, seed_up, gain_down, qkv_down, outproj_down,
    gain_up, qkv_up, outproj_up, doc_offsets, slot_order,
):
    section = lax.axis_index("section")
    sections = lax.axis_size("section")
    replica = lax.axis_index("dp")
    parts = lax.axis_size("dp")
    query_width = outproj_down.shape[1]
    model = act_down.shape[3]

    def scalars(direction, slot):
        which = slot_order[direction, 0, slot]
        offset = doc_offsets[direction, 0, which, 0]
        edge = section == (sections - 1 if direction == 0 else 0)
        return jnp.stack([which, offset, edge.astype(jnp.int32), replica]).astype(jnp.int32)

    up_one = first_pass(scalars(1, 0), act_up[0], gain_up, qkv_up[0], outproj_up[0], grad_up[0])
    up_moved = shifted(up_one[0], "section", 1)
    down_one = first_pass(scalars(0, 0), act_down[0], gain_down, qkv_down[0], outproj_down[0], grad_down[0])
    down_moved = shifted(down_one[0], "section", -1)
    up_forward = forward_pass(scalars(1, 1), act_up[0], gain_up, qkv_up[0], query_width)
    down_forward = forward_pass(scalars(0, 1), act_down[0], gain_down, qkv_down[0], query_width)
    up_out_send, up_out_keep, up_stream = outproj_pass(
        scalars(1, 1), up_one[2], up_forward[2], grad_up[0], up_moved, seed_up, parts
    )
    up_out = replica_sum(up_out_send, up_out_keep, "dp").astype(BF16)
    mirror_out = mirrored(up_out, "section")
    up_two, up_send, up_keep = second_pass(
        scalars(1, 1), act_up[0], up_forward, up_one, up_stream, gain_up, qkv_up[0], outproj_up[0], parts
    )
    up_qkv = replica_sum(up_send, up_keep, "dp").astype(BF16)
    mirror_qkv = mirrored(up_qkv, "section")
    down_out_send, down_out_keep, down_stream = outproj_pass(
        scalars(0, 1), down_one[2], down_forward[2], grad_down[0], down_moved, seed_down, parts
    )
    down_two, down_send, down_keep = second_pass(
        scalars(0, 1), act_down[0], down_forward, down_one, down_stream, gain_down, qkv_down[0], outproj_down[0], parts
    )
    down_out = replica_sum(down_out_send, down_out_keep, "dp")
    down_qkv = replica_sum(down_send, down_keep, "dp")
    rows = model // parts
    grad_outproj = down_out + mirror_out.astype(F32)
    grad_qkv = down_qkv[:rows] + mirror_qkv[:rows].astype(F32)
    grad_gain = down_qkv[rows, :rows] + mirror_qkv[rows, :rows].astype(F32)
    input_grads = jnp.stack(
        [jnp.stack([down_one[0], down_two], axis=0), jnp.stack([up_one[0], up_two], axis=0)], axis=0
    )[:, None]
    return (input_grads, grad_gain[None], grad_qkv[None], grad_outproj[None])


def solution(mesh):
    return jax.shard_map(
        shards,
        mesh=mesh,
        in_specs=(
            P("section", None, "dp", None),
            P("section", None, "dp", None),
            P("section", "dp", None),
            P("section", "dp", None),
            P("dp", None),
            P("dp", None),
            P("section", None),
            P("section", None, None),
            P("section", None, None),
            P("section", None),
            P("section", None, None),
            P("section", None, None),
            P(None, "section", None, "dp"),
            P(None, "section", None),
        ),
        out_specs=(
            P(None, "section", None, "dp", None),
            P("section", "dp"),
            P("section", "dp", None),
            P("section", "dp", None),
        ),
        check_vma=False,
    )
```

```python
import functools
import math
import jax
import jax.numpy as jnp
from jax import lax
from jax.experimental import pallas as pl
from jax.experimental.pallas import tpu as pltpu
from jax.sharding import PartitionSpec as P

HEADS = 8
KV_HEADS = 2
EPSILON = 1e-05
MASKED = -1e30
PAD = 16
PACKED_PAD = 32
PIECES = 2
PIECES_OUT = 2
PIECES_QKV = 3
VMEM_LIMIT = 24 * 1024 * 1024
FIRST_LIMIT = 60 * 1024 * 1024
F32 = jnp.float32
BF16 = jnp.bfloat16
NN = (((1,), (0,)), ((), ()))
NT = (((1,), (1,)), ((), ()))
TN = (((0,), (0,)), ((), ()))


def dot(a, b, dims=NN):
    return lax.dot_general(a, b, dims, preferred_element_type=F32)


def doubled(pair, half):
    wide = pair.astype(F32)
    turned = pltpu.roll(wide, half, 1)
    left = lax.broadcasted_iota(jnp.int32, wide.shape, 1) < half
    zero = jnp.zeros_like(wide)
    out = []
    for g in range(KV_HEADS):
        a, b = (wide, turned) if g == 0 else (turned, wide)
        out.append(
            jnp.concatenate([jnp.where(left, a, zero), jnp.where(left, zero, b)], axis=0).astype(BF16)
        )
    return out


def mask_bias(seq, offset):
    row = lax.broadcasted_iota(jnp.int32, (seq, seq), 0)
    col = lax.broadcasted_iota(jnp.int32, (seq, seq), 1)
    start = jnp.where(row >= offset, offset, 0)
    return jnp.where((col <= row) & (col >= start), 0.0, MASKED).astype(F32)


def normalise(x, gain):
    xf = x.astype(F32)
    inverse = lax.rsqrt(jnp.mean(xf * xf, axis=1, keepdims=True) + EPSILON)
    scaled = xf * inverse
    return inverse, scaled, (scaled * gain).astype(BF16)


def forward_heads(project, offset, query_width, soft_ref):
    seq = project.shape[0]
    half = query_width // HEADS
    wide = 2 * half
    keys = doubled(project[:, query_width : query_width + wide], half)
    values = doubled(project[:, query_width + wide :], half)
    bias = mask_bias(seq, offset)
    scale = half ** (-0.5)
    pairs = HEADS // 2
    attended = []
    for p in range(pairs):
        g = p * KV_HEADS // pairs
        queries = project[:, p * wide : (p + 1) * wide] * jnp.asarray(scale, BF16)
        scores = dot(queries, keys[g], NT)
        for t in range(2):
            s = scores[:, t * seq : (t + 1) * seq] + bias
            e = jnp.exp(s - jnp.max(s, axis=1, keepdims=True))
            soft = e * (1.0 / jnp.sum(e, axis=1, keepdims=True))
            soft_ref[p, :, t * seq : (t + 1) * seq] = soft.astype(BF16)
        attended.append(dot(soft_ref[p], values[g]))
    return attended


def backward_heads(project, attended, grad_attended, query_width, soft_ref):
    seq = project.shape[0]
    half = query_width // HEADS
    wide = 2 * half
    keys = doubled(project[:, query_width : query_width + wide], half)
    values = doubled(project[:, query_width + wide :], half)
    scale = half ** (-0.5)
    pairs = HEADS // 2
    left = lax.broadcasted_iota(jnp.int32, (seq, wide), 1) < half
    grad_queries = []
    grad_keys = [None] * KV_HEADS
    grad_values = [None] * KV_HEADS
    for p in range(pairs):
        g = p * KV_HEADS // pairs
        queries = project[:, p * wide : (p + 1) * wide] * jnp.asarray(scale, BF16)
        grad_pair = grad_attended[:, p * wide : (p + 1) * wide]
        grad_soft = dot(grad_pair, values[g], NT)
        both = attended[p].astype(F32) * grad_pair.astype(F32)
        rows = [
            jnp.sum(jnp.where(left, both, 0.0), axis=1, keepdims=True),
            jnp.sum(jnp.where(left, 0.0, both), axis=1, keepdims=True),
        ]
        soft = soft_ref[p]
        grad_scores = jnp.concatenate(
            [
                (
                    soft[:, t * seq : (t + 1) * seq].astype(F32)
                    * (grad_soft[:, t * seq : (t + 1) * seq] - rows[t])
                ).astype(BF16)
                for t in range(2)
            ],
            axis=1,
        )
        grad_queries.append(dot(grad_scores, keys[g]) * scale)
        keys_part = dot(queries, grad_scores, TN)
        values_part = dot(grad_pair, soft, TN)
        keys_sum = keys_part[:half, :seq] + keys_part[half:, seq:]
        values_sum = values_part[:half, :seq] + values_part[half:, seq:]
        grad_keys[g] = keys_sum if grad_keys[g] is None else grad_keys[g] + keys_sum
        grad_values[g] = values_sum if grad_values[g] is None else grad_values[g] + values_sum
    columns = grad_queries + [
        jnp.concatenate(grad_keys, axis=0).T,
        jnp.concatenate(grad_values, axis=0).T,
    ]
    return jnp.concatenate([c.astype(BF16) for c in columns], axis=1)


def input_gradient(grad_project, qkv, gain, scaled, inverse, upstream):
    grad_normed = dot(grad_project, qkv, NT)
    grad_hat = grad_normed * gain
    part = grad_normed * scaled
    grad_gain = jnp.sum(part, axis=0, keepdims=True)
    mean = jnp.mean(part * gain, axis=1, keepdims=True)
    grad_in = upstream.astype(F32) + inverse * (grad_hat - scaled * mean)
    return grad_in.astype(BF16), grad_gain


def whole(memory=pltpu.VMEM):
    return pl.BlockSpec(memory_space=memory)


def call(kernel, name, inputs, outputs, scratch, after=(), aliases=None, limit=VMEM_LIMIT):
    count = len(inputs)

    def ordered(*refs):
        kernel(*refs[:count], *refs[count + len(after) :])

    return pl.pallas_call(
        ordered,
        out_shape=tuple(jax.ShapeDtypeStruct(shape, dtype) for shape, dtype, _ in outputs),
        in_specs=[whole(space) for _, space in inputs] + [whole(pl.ANY)] * len(after),
        out_specs=tuple(whole(space) for _, _, space in outputs),
        scratch_shapes=scratch,
        input_output_aliases=aliases or {},
        compiler_params=pltpu.CompilerParams(vmem_limit_bytes=limit),
        cost_estimate=pl.CostEstimate(flops=1, bytes_accessed=1, transcendentals=0),
        name=name,
    )(*(array for array, _ in inputs), *after)


def start_all(sources, targets, sems):
    copies = [pltpu.make_async_copy(a, b, sems.at[i]) for i, (a, b) in enumerate(zip(sources, targets))]
    for copy in copies:
        copy.start()
    return copies


def first_kernel(order, offsets, act, qkv_hbm, out_hbm, up_hbm, gain_hbm, *refs, direction):
    grad_ref, normed_ref, attended_ref, project_ref, gain_out = refs[:5]
    order_ref, offsets_ref, x_ref, qkv_ref, out_ref, up_ref, gain_ref, soft_ref, sems = refs[5:]
    copies = start_all(
        (order, offsets, act, gain_hbm, qkv_hbm, up_hbm, out_hbm),
        (order_ref, offsets_ref, x_ref, gain_ref, qkv_ref, up_ref, out_ref),
        sems,
    )
    query_width = out_hbm.shape[0]
    for copy in copies[:4]:
        copy.wait()
    which = order_ref[direction, 0, 0]
    offset = offsets_ref[direction, 0, which]
    gain = gain_ref[...]
    _, _, normed = normalise(x_ref[which], gain)
    normed_ref[...] = normed
    copies[4].wait()
    project = dot(normed, qkv_ref[...]).astype(BF16)
    attended = forward_heads(project, offset, query_width, soft_ref)
    attended_ref[...] = jnp.concatenate([a.astype(BF16) for a in attended], axis=1)
    copies[5].wait()
    copies[6].wait()
    grad_attended = dot(up_ref[...], out_ref[...], NT).astype(BF16)
    grad_project = backward_heads(project, attended, grad_attended, query_width, soft_ref)
    project_ref[...] = grad_project
    inverse, scaled, _ = normalise(x_ref[which], gain)
    grad_ref[...], gain_out[...] = input_gradient(grad_project, qkv_ref[...], gain, scaled, inverse, up_ref[...])


def first_pass(direction, ints, act, gain, qkv, out, upstream, after=(), limit=VMEM_LIMIT):
    seq, model = act.shape[1:]
    width = qkv.shape[1]
    query_width = out.shape[0]
    hbm, vmem = pltpu.HBM, pltpu.VMEM
    return call(
        functools.partial(first_kernel, direction=direction),
        "first_pass",
        [(a, hbm) for a in (*ints, act, qkv, out, upstream, gain)],
        [
            ((seq, model), BF16, vmem),
            ((seq, model), BF16, vmem),
            ((seq, query_width), BF16, vmem),
            ((seq, width), BF16, vmem),
            ((1, model), F32, vmem),
        ],
        [pltpu.SMEM(a.shape, jnp.int32) for a in ints]
        + [
            pltpu.VMEM(act.shape, BF16),
            pltpu.VMEM((model, width), BF16),
            pltpu.VMEM((query_width, model), BF16),
            pltpu.VMEM((seq, model), BF16),
            pltpu.VMEM((1, model), F32),
            pltpu.VMEM((HEADS // 2, seq, 2 * seq), BF16),
            pltpu.SemaphoreType.DMA((7,)),
        ],
        after,
        limit=limit,
    )


def forward_kernel(order, offsets, act, qkv_hbm, gain_hbm, *refs, direction, query_width):
    normed_ref, project_ref, attended_ref, soft_ref = refs[:4]
    order_ref, offsets_ref, x_ref, qkv_ref, gain_ref, sems = refs[4:]
    copies = start_all(
        (order, offsets, act, gain_hbm, qkv_hbm), (order_ref, offsets_ref, x_ref, gain_ref, qkv_ref), sems
    )
    for copy in copies[:4]:
        copy.wait()
    which = order_ref[direction, 0, 1]
    offset = offsets_ref[direction, 0, which]
    _, _, normed = normalise(x_ref[which], gain_ref[...])
    normed_ref[...] = normed
    copies[4].wait()
    project = dot(normed, qkv_ref[...]).astype(BF16)
    project_ref[...] = project
    attended = forward_heads(project, offset, query_width, soft_ref)
    attended_ref[...] = jnp.concatenate([a.astype(BF16) for a in attended], axis=1)


def forward_pass(direction, ints, act, gain, qkv, query_width, after=()):
    seq, model = act.shape[1:]
    width = qkv.shape[1]
    hbm, vmem = pltpu.HBM, pltpu.VMEM
    return call(
        functools.partial(forward_kernel, direction=direction, query_width=query_width),
        "forward_pass",
        [(a, hbm) for a in (*ints, act, qkv, gain)],
        [
            ((seq, model), BF16, vmem),
            ((seq, width), BF16, vmem),
            ((seq, query_width), BF16, vmem),
            ((HEADS // 2, seq, 2 * seq), BF16, vmem),
        ],
        [pltpu.SMEM(a.shape, jnp.int32) for a in ints]
        + [
            pltpu.VMEM(act.shape, BF16),
            pltpu.VMEM((model, width), BF16),
            pltpu.VMEM((1, model), F32),
            pltpu.SemaphoreType.DMA((5,)),
        ],
        after,
    )


def choose_upstream(direction, moved, seed_hbm, up_ref, sem):
    seeded = lax.axis_index("section") == (lax.axis_size("section") - 1 if direction == 0 else 0)

    @pl.when(seeded)
    def _():
        copy = pltpu.make_async_copy(seed_hbm, up_ref, sem)
        copy.start()
        copy.wait()

    @pl.when(jnp.logical_not(seeded))
    def _():
        up_ref[...] = moved[...]


def backward_kernel(
    order, act, qkv_hbm, out_hbm, gain_hbm, seed_hbm, project_ref, attended_ref, soft_ref, gain1, moved, own,
    *refs, direction, kept,
):
    up_ref, gproj_ref, gain_out, grads_hbm = refs[kept : kept + 4]
    order_ref, x_ref, qkv_ref, out_ref, gain_ref, grad_ref, sems = refs[kept + 4 :]
    copies = start_all(
        (order, act, gain_hbm, out_hbm, qkv_hbm), (order_ref, x_ref, gain_ref, out_ref, qkv_ref), sems
    )
    choose_upstream(direction, moved, seed_hbm, up_ref, sems.at[5])
    copies[3].wait()
    query_width = out_ref.shape[0]
    wide = 2 * query_width // HEADS
    grad_attended = dot(up_ref[...], out_ref[...], NT).astype(BF16)
    attended = [attended_ref[:, p * wide : (p + 1) * wide] for p in range(HEADS // 2)]
    gproj_ref[...] = backward_heads(project_ref[...], attended, grad_attended, query_width, soft_ref)
    for at in (0, 1, 2, 4):
        copies[at].wait()
    gain = gain_ref[...]
    inverse, scaled, _ = normalise(x_ref[order_ref[direction, 0, 1]], gain)
    grad_ref[0] = own[...]
    grad_ref[1], grad_gain = input_gradient(gproj_ref[...], qkv_ref[...], gain, scaled, inverse, up_ref[...])
    gain_out[...] = gain1[...] + grad_gain
    written = pltpu.make_async_copy(grad_ref, grads_hbm.at[direction], sems.at[6])
    written.start()
    written.wait()


def backward_pass(direction, order, act, gain, qkv, out, seed, forward, gain1, moved, own, grads=None, after=()):
    seq, model = act.shape[1:]
    width = qkv.shape[1]
    query_width = out.shape[0]
    hbm, vmem = pltpu.HBM, pltpu.VMEM
    _, project, attended, soft = forward
    inputs = [(a, hbm) for a in (order, act, qkv, out, gain, seed)]
    inputs += [(a, vmem) for a in (project, attended, soft, gain1, moved, own)]
    aliases = {}
    if grads is not None:
        aliases = {len(inputs): 3}
        inputs += [(grads, hbm)]
    return call(
        functools.partial(backward_kernel, direction=direction, kept=len(aliases)),
        "backward_pass",
        inputs,
        [
            ((seq, model), BF16, vmem),
            ((seq, width), BF16, vmem),
            ((1, model), F32, vmem),
            ((2, 2, seq, model), BF16, hbm),
        ],
        [
            pltpu.SMEM(order.shape, jnp.int32),
            pltpu.VMEM(act.shape, BF16),
            pltpu.VMEM((model, width), BF16),
            pltpu.VMEM((query_width, model), BF16),
            pltpu.VMEM((1, model), F32),
            pltpu.VMEM((2, seq, model), BF16),
            pltpu.SemaphoreType.DMA((7,)),
        ],
        after,
        aliases,
    )


def cut(rows, pieces):
    return max(p for p in range(1, pieces + 1) if rows % (16 * p) == 0)


def hand_out(blocks, sends, keep_ref):
    parts = blocks.shape[0]
    replica = lax.axis_index("dp")
    for k in range(parts - 1):
        at = lax.rem(replica + 1 + k, parts)
        for p, ref in enumerate(sends):
            rows = ref.shape[1]
            ref[k] = blocks[at, p * rows : (p + 1) * rows, :]
    keep_ref[...] = blocks[replica]


def outproj_kernel(up_hbm, seed_hbm, att1, att2, moved, *refs, direction):
    *sends, keep_ref, up1_ref, up2_ref, blocks, sems = refs
    copy = pltpu.make_async_copy(up_hbm, up1_ref, sems.at[0])
    copy.start()
    choose_upstream(direction, moved, seed_hbm, up2_ref, sems.at[1])
    parts, rows, _ = blocks.shape
    copy.wait()
    total = dot(att1[...], up1_ref[...], TN) + dot(att2[...], up2_ref[...], TN)
    for q in range(parts):
        blocks[q] = total[q * rows : (q + 1) * rows].astype(BF16)
    hand_out(blocks, sends, keep_ref)


def outproj_pass(direction, att1, att2, upstream, moved, seed, parts, after=()):
    seq, model = moved.shape
    rows = att1.shape[1] // parts
    pieces = cut(rows, PIECES_OUT)
    hbm, vmem = pltpu.HBM, pltpu.VMEM
    *sends, keep = call(
        functools.partial(outproj_kernel, direction=direction),
        "outproj_pass",
        [(upstream, hbm), (seed, hbm), (att1, vmem), (att2, vmem), (moved, vmem)],
        [((parts - 1, rows // pieces, model), BF16, vmem)] * pieces + [((rows, model), BF16, vmem)],
        [
            pltpu.VMEM((seq, model), BF16),
            pltpu.VMEM((seq, model), BF16),
            pltpu.VMEM((parts, rows, model), BF16),
            pltpu.SemaphoreType.DMA((2,)),
        ],
        after,
    )
    return sends, keep


def qkv_kernel(normed1, gproj1, normed2, gproj2, gain, *refs):
    *sends, keep_ref, blocks = refs
    parts, height, width = blocks.shape
    rows = normed1.shape[1] // parts
    for q in range(parts):
        at = slice(q * rows, (q + 1) * rows)
        total = dot(normed1[:, at], gproj1[...], TN) + dot(normed2[:, at], gproj2[...], TN)
        blocks[q, :rows, :] = total.astype(BF16)
        blocks[q, rows:, :] = jnp.zeros((height - rows, width), BF16)
        blocks[q, rows:, :rows] = jnp.broadcast_to(gain[:, at], (height - rows, rows)).astype(BF16)
    hand_out(blocks, sends, keep_ref)


def qkv_pass(normed1, gproj1, normed2, gproj2, gain, parts, after=()):
    rows, width = normed1.shape[1] // parts + PAD, gproj1.shape[1]
    pieces = cut(rows, PIECES_QKV)
    vmem = pltpu.VMEM
    *sends, keep = call(
        qkv_kernel,
        "qkv_pass",
        [(a, vmem) for a in (normed1, gproj1, normed2, gproj2, gain)],
        [((parts - 1, rows // pieces, width), BF16, vmem)] * pieces + [((rows, width), BF16, vmem)],
        [pltpu.VMEM((parts, rows, width), BF16)],
        after,
    )
    return sends, keep


def layout(parts, query_width, model, width):
    unit = math.gcd(model, width)
    out_rows, qkv_rows = query_width // parts, model // parts
    start = out_rows * (model // unit)
    gain_at = start + qkv_rows * (width // unit)
    return unit, out_rows, qkv_rows, start, gain_at, gain_at + PACKED_PAD


def packed_kernel(normed1, gproj1, att1, up1_hbm, normed2, gproj2, att2, up2, gain, *refs):
    *sends, keep_ref, blocks, up1, sem = refs
    copy = pltpu.make_async_copy(up1_hbm, up1, sem)
    copy.start()
    parts = blocks.shape[0]
    model, width = normed1.shape[1], gproj1.shape[1]
    unit, out_rows, qkv_rows, start, gain_at, _ = layout(parts, att1.shape[1], model, width)
    row = lax.broadcasted_iota(jnp.int32, (PACKED_PAD, unit), 0)
    for q in range(parts):
        at = slice(q * qkv_rows, (q + 1) * qkv_rows)
        qkv = dot(normed1[:, at], gproj1[...], TN) + dot(normed2[:, at], gproj2[...], TN)
        for c in range(width // unit):
            first = start + c * qkv_rows
            blocks[q, first : first + qkv_rows, :] = qkv[:, c * unit : (c + 1) * unit].astype(BF16)
        lines = jnp.zeros((PACKED_PAD, unit), F32)
        for i in range(pl.cdiv(qkv_rows, unit)):
            line = gain[:, q * qkv_rows + i * unit : q * qkv_rows + min((i + 1) * unit, qkv_rows)]
            if line.shape[1] < unit:
                line = jnp.concatenate([line, jnp.zeros((1, unit - line.shape[1]), F32)], axis=1)
            lines = jnp.where(row == i, line, lines)
        blocks[q, gain_at:, :] = lines.astype(BF16)
    copy.wait()
    out = dot(att1[...], up1[...], TN) + dot(att2[...], up2[...], TN)
    for q in range(parts):
        for c in range(model // unit):
            blocks[q, c * out_rows : (c + 1) * out_rows, :] = out[
                q * out_rows : (q + 1) * out_rows, c * unit : (c + 1) * unit
            ].astype(BF16)
    hand_out(blocks, sends, keep_ref)


def packed_pass(normed1, gproj1, att1, up1, normed2, gproj2, att2, up2, gain, parts, after=()):
    seq, model = normed1.shape
    unit, _, _, _, _, rows = layout(parts, att1.shape[1], model, gproj1.shape[1])
    pieces = cut(rows, PIECES)
    hbm, vmem = pltpu.HBM, pltpu.VMEM
    *sends, keep = call(
        packed_kernel,
        "packed_pass",
        [(normed1, vmem), (gproj1, vmem), (att1, vmem), (up1, hbm)]
        + [(a, vmem) for a in (normed2, gproj2, att2, up2, gain)],
        [((parts - 1, rows // pieces, unit), BF16, vmem)] * pieces + [((rows, unit), BF16, vmem)],
        [
            pltpu.VMEM((parts, rows, unit), BF16),
            pltpu.VMEM((seq, model), BF16),
            pltpu.SemaphoreType.DMA(()),
        ],
        after,
    )
    return sends, keep


def final_kernel(keep, mirror_out, mirror_qkv, *refs, parts, pieces):
    moved, refs = refs[: (parts - 1) * pieces], refs[(parts - 1) * pieces :]
    gain_hbm, qkv_hbm, out_hbm, gain_ref, qkv_ref, out_ref, sems = refs
    model, width = out_ref.shape[1], qkv_ref.shape[1]
    unit, out_rows, qkv_rows, start, gain_at, rows = layout(parts, out_ref.shape[0] * parts, model, width)
    each = rows // pieces

    def total(first, count):
        result = keep[first : first + count, :].astype(F32)
        for k in range(parts - 1):
            taken, at = [], first
            while at < first + count:
                p = at // each
                until = min(first + count, (p + 1) * each)
                taken.append(moved[k * pieces + p][at - p * each : until - p * each, :].astype(F32))
                at = until
            result = result + (taken[0] if len(taken) == 1 else jnp.concatenate(taken, axis=0))
        return result

    for c in range(width // unit):
        columns = slice(c * unit, (c + 1) * unit)
        qkv_ref[:, columns] = total(start + c * qkv_rows, qkv_rows) + mirror_qkv[:qkv_rows, columns].astype(F32)
    copies = [pltpu.make_async_copy(qkv_ref, qkv_hbm, sems.at[0])]
    copies[0].start()
    for c in range(model // unit):
        columns = slice(c * unit, (c + 1) * unit)
        out_ref[:, columns] = total(c * out_rows, out_rows) + mirror_out[:, columns].astype(F32)
    copies.append(pltpu.make_async_copy(out_ref, out_hbm, sems.at[1]))
    copies[1].start()
    lines = total(gain_at, PACKED_PAD)
    other = mirror_qkv[qkv_rows:, :].astype(F32)
    for i in range(pl.cdiv(qkv_rows, unit)):
        until = min((i + 1) * unit, qkv_rows)
        gain_ref[:, i * unit : until] = lines[i : i + 1, : until - i * unit] + other[:1, i * unit : until]
    copies.append(pltpu.make_async_copy(gain_ref, gain_hbm, sems.at[2]))
    copies[2].start()
    for copy in copies:
        copy.wait()


def final_pass(keep, mirror_out, mirror_qkv, moved, parts, query_width, model, width):
    hbm, vmem = pltpu.HBM, pltpu.VMEM
    shapes = ((1, model // parts), (model // parts, width), (query_width // parts, model))
    return call(
        functools.partial(final_kernel, parts=parts, pieces=len(moved[0])),
        "final_pass",
        [(keep, vmem), (mirror_out, vmem), (mirror_qkv, vmem)] + [(m, vmem) for per in moved for m in per],
        [(shape, F32, hbm) for shape in shapes],
        [pltpu.VMEM(shape, F32) for shape in shapes] + [pltpu.SemaphoreType.DMA((3,))],
    )


def sum_kernel(keep, *refs):
    *moved, sum_ref = refs
    pieces = len(moved)
    at = 0
    for p in range(pieces):
        rows = moved[p].shape[1]
        total = keep[at : at + rows, :].astype(F32)
        for k in range(moved[p].shape[0]):
            total = total + moved[p][k].astype(F32)
        sum_ref[at : at + rows, :] = total.astype(BF16)
        at += rows


def sum_pass(keep, moved, after=()):
    vmem = pltpu.VMEM
    pieces = [jnp.stack([per[p] for per in moved]) if len(moved) > 1 else moved[0][p][None] for p in range(len(moved[0]))]
    (total,) = call(
        sum_kernel, "sum_pass", [(keep, vmem)] + [(p, vmem) for p in pieces], [(keep.shape, BF16, vmem)], [], after
    )
    return total


def shifted(value, axis, steps):
    count = lax.axis_size(axis)
    first, last = (max(0, -steps), min(count, count - steps))
    return lax.ppermute(value, axis, [(source, source + steps) for source in range(first, last)])


def mirrored(value, axis):
    count = lax.axis_size(axis)
    return lax.ppermute(value, axis, [(i, count - 1 - i) for i in range(count)])


def exchanged(sends, axis):
    parts = lax.axis_size(axis)
    return [
        [lax.ppermute(send[k], axis, [(i, (i + 1 + k) % parts) for i in range(parts)]) for send in sends]
        for k in range(parts - 1)
    ]


def shards(
    act_down, act_up, grad_down, grad_up, seed_down, seed_up, gain_down, qkv_down, outproj_down,
    gain_up, qkv_up, outproj_up, doc_offsets, slot_order,
):
    parts = lax.axis_size("dp")
    query_width, model = outproj_down.shape[1:]
    width = qkv_down.shape[2]
    ints = (slot_order, doc_offsets.reshape(slot_order.shape))
    down = (gain_down, qkv_down[0], outproj_down[0])
    up = (gain_up, qkv_up[0], outproj_up[0])

    up_one = first_pass(1, ints, act_up[0], *up, grad_up[0], limit=FIRST_LIMIT)
    up_moved = shifted(up_one[0], "section", 1)
    down_one = first_pass(0, ints, act_down[0], *down, grad_down[0], after=(up_one[3],))
    down_moved = shifted(down_one[0], "section", -1)
    up_forward = forward_pass(1, ints, act_up[0], gain_up, qkv_up[0], query_width, after=(down_one[3],))
    sends, keep = outproj_pass(1, up_one[2], up_forward[2], grad_up[0], up_moved, seed_up, parts)
    up_out = sum_pass(keep, exchanged(sends, "dp"))
    mirror_out = mirrored(up_out, "section")
    up_two = backward_pass(
        1, slot_order, act_up[0], *up, seed_up, up_forward, up_one[4], up_moved, up_one[0], after=(up_out,)
    )
    sends, keep = qkv_pass(up_one[1], up_one[3], up_forward[0], up_two[1], up_two[2], parts, after=(down_moved,))
    up_qkv = sum_pass(keep, exchanged(sends, "dp"), after=(mirror_out,))
    mirror_qkv = mirrored(up_qkv, "section")
    down_forward = forward_pass(0, ints, act_down[0], gain_down, qkv_down[0], query_width, after=(keep,))
    down_two = backward_pass(
        0, slot_order, act_down[0], *down, seed_down, down_forward, down_one[4], down_moved, down_one[0],
        grads=up_two[3], after=(up_qkv,),
    )
    sends, keep = packed_pass(
        down_one[1], down_one[3], down_one[2], grad_down[0],
        down_forward[0], down_two[1], down_forward[2], down_two[0], down_two[2], parts,
    )
    grad_gain, grad_qkv, grad_outproj = final_pass(
        keep, mirror_out, mirror_qkv, exchanged(sends, "dp"), parts, query_width, model, width
    )
    return (down_two[3][:, None], grad_gain, grad_qkv[None], grad_outproj[None])


def solution(mesh):
    return jax.shard_map(
        shards,
        mesh=mesh,
        in_specs=(
            P("section", None, "dp", None),
            P("section", None, "dp", None),
            P("section", "dp", None),
            P("section", "dp", None),
            P("dp", None),
            P("dp", None),
            P("section", None),
            P("section", None, None),
            P("section", None, None),
            P("section", None),
            P("section", None, None),
            P("section", None, None),
            P(None, "section", None, "dp"),
            P(None, "section", None),
        ),
        out_specs=(
            P(None, "section", None, "dp", None),
            P("section", "dp"),
            P("section", "dp", None),
            P("section", "dp", None),
        ),
        check_vma=False,
    )
```

```python
import functools
import math
import jax
import jax.numpy as jnp
from jax import lax
from jax.experimental import pallas as pl
from jax.experimental.pallas import tpu as pltpu
from jax.sharding import PartitionSpec as P

HEADS = 8
KV_HEADS = 2
EPSILON = 1e-05
MASKED = -1e30
PAD = 16
PACKED_PAD = 32
PIECES = 2
PIECES_OUT = 2
PIECES_QKV = 3
VMEM_LIMIT = 24 * 1024 * 1024
FIRST_LIMIT = 60 * 1024 * 1024
F32 = jnp.float32
BF16 = jnp.bfloat16
NN = (((1,), (0,)), ((), ()))
NT = (((1,), (1,)), ((), ()))
TN = (((0,), (0,)), ((), ()))


def dot(a, b, dims=NN):
    return lax.dot_general(a, b, dims, preferred_element_type=F32)


def doubled(pair, half):
    wide = pair.astype(F32)
    turned = pltpu.roll(wide, half, 1)
    left = lax.broadcasted_iota(jnp.int32, wide.shape, 1) < half
    zero = jnp.zeros_like(wide)
    out = []
    for g in range(KV_HEADS):
        a, b = (wide, turned) if g == 0 else (turned, wide)
        out.append(
            jnp.concatenate([jnp.where(left, a, zero), jnp.where(left, zero, b)], axis=0).astype(BF16)
        )
    return out


def mask_bias(seq, offset):
    row = lax.broadcasted_iota(jnp.int32, (seq, seq), 0)
    col = lax.broadcasted_iota(jnp.int32, (seq, seq), 1)
    start = jnp.where(row >= offset, offset, 0)
    return jnp.where((col <= row) & (col >= start), 0.0, MASKED).astype(F32)


def normalise(x, gain):
    xf = x.astype(F32)
    inverse = lax.rsqrt(jnp.mean(xf * xf, axis=1, keepdims=True) + EPSILON)
    scaled = xf * inverse
    return inverse, scaled, (scaled * gain).astype(BF16)


def softmax(scores):
    e = jnp.exp(scores - jnp.max(scores, axis=1, keepdims=True))
    return (e * (1.0 / jnp.sum(e, axis=1, keepdims=True))).astype(BF16)


def pair_columns(array, query_width):
    wide = 2 * (query_width // HEADS)
    return [array[:, p * wide : (p + 1) * wide] for p in range(HEADS // 2)]


def forward_heads(project, offset, query_width, soft_ref):
    seq = project.shape[0]
    half = query_width // HEADS
    wide = 2 * half
    keys = doubled(project[:, query_width : query_width + wide], half)
    values = doubled(project[:, query_width + wide :], half)
    bias = mask_bias(seq, offset)
    scale = jnp.asarray(half ** (-0.5), BF16)
    pairs = HEADS // 2
    group = [p * KV_HEADS // pairs for p in range(pairs)]
    queries = pair_columns(project, query_width)
    scores = [dot(queries[p] * scale, keys[group[p]], NT) for p in range(pairs)]
    for p in range(pairs):
        for t in range(2):
            at = slice(t * seq, (t + 1) * seq)
            soft_ref[p, :, at] = softmax(scores[p][:, at] + bias)
    return [dot(soft_ref[p], values[group[p]]) for p in range(pairs)]


def backward_heads(project, attended, grad_attended, query_width, soft_ref):
    seq = project.shape[0]
    half = query_width // HEADS
    wide = 2 * half
    keys = doubled(project[:, query_width : query_width + wide], half)
    values = doubled(project[:, query_width + wide :], half)
    scale = half ** (-0.5)
    pairs = HEADS // 2
    group = [p * KV_HEADS // pairs for p in range(pairs)]
    left = lax.broadcasted_iota(jnp.int32, (seq, wide), 1) < half
    queries = [q * jnp.asarray(scale, BF16) for q in pair_columns(project, query_width)]
    grads = pair_columns(grad_attended, query_width)
    grad_soft = [dot(grads[p], values[group[p]], NT) for p in range(pairs)]
    values_parts = [dot(grads[p], soft_ref[p], TN) for p in range(pairs)]
    grad_scores = []
    for p in range(pairs):
        both = attended[p].astype(F32) * grads[p].astype(F32)
        rows = [
            jnp.sum(jnp.where(left, both, 0.0), axis=1, keepdims=True),
            jnp.sum(jnp.where(left, 0.0, both), axis=1, keepdims=True),
        ]
        columns = [slice(t * seq, (t + 1) * seq) for t in range(2)]
        grad_scores.append(
            jnp.concatenate(
                [
                    (soft_ref[p, :, at].astype(F32) * (grad_soft[p][:, at] - row)).astype(BF16)
                    for at, row in zip(columns, rows)
                ],
                axis=1,
            )
        )
    grad_queries = [dot(grad_scores[p], keys[group[p]]) * scale for p in range(pairs)]
    keys_parts = [dot(queries[p], grad_scores[p], TN) for p in range(pairs)]

    def joined(parts):
        sums = []
        for g in range(KV_HEADS):
            part = sum(parts[p] for p in range(pairs) if group[p] == g)
            sums.append(part[:half, :seq] + part[half:, seq:])
        return jnp.concatenate(sums, axis=0).T

    columns = [*grad_queries, joined(keys_parts), joined(values_parts)]
    return jnp.concatenate([c.astype(BF16) for c in columns], axis=1)


def input_gradient(grad_project, qkv, gain, scaled, inverse, upstream):
    grad_normed = dot(grad_project, qkv, NT)
    grad_hat = grad_normed * gain
    part = grad_normed * scaled
    grad_gain = jnp.sum(part, axis=0, keepdims=True)
    mean = jnp.mean(part * gain, axis=1, keepdims=True)
    grad_in = upstream.astype(F32) + inverse * (grad_hat - scaled * mean)
    return grad_in.astype(BF16), grad_gain


def whole(memory=pltpu.VMEM):
    return pl.BlockSpec(memory_space=memory)


def call(kernel, name, inputs, outputs, scratch, after=(), aliases=None, limit=VMEM_LIMIT):
    count = len(inputs)

    def ordered(*refs):
        kernel(*refs[:count], *refs[count + len(after) :])

    return pl.pallas_call(
        ordered,
        out_shape=tuple(jax.ShapeDtypeStruct(shape, dtype) for shape, dtype, _ in outputs),
        in_specs=[whole(space) for _, space in inputs] + [whole(pl.ANY)] * len(after),
        out_specs=tuple(whole(space) for _, _, space in outputs),
        scratch_shapes=scratch,
        input_output_aliases=aliases or {},
        compiler_params=pltpu.CompilerParams(vmem_limit_bytes=limit),
        cost_estimate=pl.CostEstimate(flops=1, bytes_accessed=1, transcendentals=0),
        name=name,
    )(*(array for array, _ in inputs), *after)


def start_all(sources, targets, sems):
    copies = [pltpu.make_async_copy(a, b, sems.at[i]) for i, (a, b) in enumerate(zip(sources, targets))]
    for copy in copies:
        copy.start()
    return copies


def first_kernel(order, offsets, act, qkv_hbm, out_hbm, up_hbm, gain_hbm, *refs, direction):
    grad_ref, normed_ref, attended_ref, project_ref, gain_out = refs[:5]
    order_ref, offsets_ref, x_ref, qkv_ref, out_ref, up_ref, gain_ref, soft_ref, sems = refs[5:]
    sources = (order, offsets, gain_hbm, act, qkv_hbm, up_hbm, out_hbm)
    targets = (order_ref, offsets_ref, gain_ref, x_ref, qkv_ref, up_ref, out_ref)
    copies = [pltpu.make_async_copy(a, b, sems.at[i]) for i, (a, b) in enumerate(zip(sources, targets))]
    for copy in copies[:5]:
        copy.start()
    query_width = out_hbm.shape[0]
    for copy in copies[:4]:
        copy.wait()
    for copy in copies[5:]:
        copy.start()
    which = order_ref[direction, 0, 0]
    offset = offsets_ref[direction, 0, which]
    gain = gain_ref[...]
    _, _, normed = normalise(x_ref[which], gain)
    normed_ref[...] = normed
    copies[4].wait()
    project = dot(normed, qkv_ref[...]).astype(BF16)
    attended = forward_heads(project, offset, query_width, soft_ref)
    attended_ref[...] = jnp.concatenate([a.astype(BF16) for a in attended], axis=1)
    copies[5].wait()
    copies[6].wait()
    grad_attended = dot(up_ref[...], out_ref[...], NT).astype(BF16)
    grad_project = backward_heads(project, attended, grad_attended, query_width, soft_ref)
    project_ref[...] = grad_project
    inverse, scaled, _ = normalise(x_ref[which], gain)
    grad_ref[...], gain_out[...] = input_gradient(grad_project, qkv_ref[...], gain, scaled, inverse, up_ref[...])


def first_pass(direction, ints, act, gain, qkv, out, upstream, after=(), limit=VMEM_LIMIT):
    seq, model = act.shape[1:]
    width = qkv.shape[1]
    query_width = out.shape[0]
    hbm, vmem = pltpu.HBM, pltpu.VMEM
    return call(
        functools.partial(first_kernel, direction=direction),
        "first_pass",
        [(a, hbm) for a in (*ints, act, qkv, out, upstream, gain)],
        [
            ((seq, model), BF16, vmem),
            ((seq, model), BF16, vmem),
            ((seq, query_width), BF16, vmem),
            ((seq, width), BF16, vmem),
            ((1, model), F32, vmem),
        ],
        [pltpu.SMEM(a.shape, jnp.int32) for a in ints]
        + [
            pltpu.VMEM(act.shape, BF16),
            pltpu.VMEM((model, width), BF16),
            pltpu.VMEM((query_width, model), BF16),
            pltpu.VMEM((seq, model), BF16),
            pltpu.VMEM((1, model), F32),
            pltpu.VMEM((HEADS // 2, seq, 2 * seq), BF16),
            pltpu.SemaphoreType.DMA((7,)),
        ],
        after,
        limit=limit,
    )


def forward_kernel(order, offsets, act, qkv_hbm, gain_hbm, *refs, direction, query_width):
    normed_ref, project_ref, attended_ref, soft_ref = refs[:4]
    order_ref, offsets_ref, x_ref, qkv_ref, gain_ref, sems = refs[4:]
    copies = start_all(
        (order, offsets, act, gain_hbm, qkv_hbm), (order_ref, offsets_ref, x_ref, gain_ref, qkv_ref), sems
    )
    for copy in copies[:4]:
        copy.wait()
    which = order_ref[direction, 0, 1]
    offset = offsets_ref[direction, 0, which]
    _, _, normed = normalise(x_ref[which], gain_ref[...])
    normed_ref[...] = normed
    copies[4].wait()
    project = dot(normed, qkv_ref[...]).astype(BF16)
    project_ref[...] = project
    attended = forward_heads(project, offset, query_width, soft_ref)
    attended_ref[...] = jnp.concatenate([a.astype(BF16) for a in attended], axis=1)


def forward_pass(direction, ints, act, gain, qkv, query_width, after=()):
    seq, model = act.shape[1:]
    width = qkv.shape[1]
    hbm, vmem = pltpu.HBM, pltpu.VMEM
    return call(
        functools.partial(forward_kernel, direction=direction, query_width=query_width),
        "forward_pass",
        [(a, hbm) for a in (*ints, act, qkv, gain)],
        [
            ((seq, model), BF16, vmem),
            ((seq, width), BF16, vmem),
            ((seq, query_width), BF16, vmem),
            ((HEADS // 2, seq, 2 * seq), BF16, vmem),
        ],
        [pltpu.SMEM(a.shape, jnp.int32) for a in ints]
        + [
            pltpu.VMEM(act.shape, BF16),
            pltpu.VMEM((model, width), BF16),
            pltpu.VMEM((1, model), F32),
            pltpu.SemaphoreType.DMA((5,)),
        ],
        after,
    )


def choose_upstream(direction, moved, seed_hbm, up_ref, sem):
    seeded = lax.axis_index("section") == (lax.axis_size("section") - 1 if direction == 0 else 0)

    @pl.when(seeded)
    def _():
        copy = pltpu.make_async_copy(seed_hbm, up_ref, sem)
        copy.start()
        copy.wait()

    @pl.when(jnp.logical_not(seeded))
    def _():
        up_ref[...] = moved[...]


def backward_kernel(
    order, act, qkv_hbm, out_hbm, gain_hbm, seed_hbm, project_ref, attended_ref, soft_ref, gain1, moved, own,
    *refs, direction, kept,
):
    up_ref, gproj_ref, gain_out, grads_hbm = refs[kept : kept + 4]
    order_ref, x_ref, qkv_ref, out_ref, gain_ref, grad_ref, sems = refs[kept + 4 :]
    copies = start_all(
        (order, act, gain_hbm, out_hbm, qkv_hbm), (order_ref, x_ref, gain_ref, out_ref, qkv_ref), sems
    )
    choose_upstream(direction, moved, seed_hbm, up_ref, sems.at[5])
    copies[3].wait()
    query_width = out_ref.shape[0]
    wide = 2 * query_width // HEADS
    grad_attended = dot(up_ref[...], out_ref[...], NT).astype(BF16)
    attended = [attended_ref[:, p * wide : (p + 1) * wide] for p in range(HEADS // 2)]
    gproj_ref[...] = backward_heads(project_ref[...], attended, grad_attended, query_width, soft_ref)
    for at in (0, 1, 2, 4):
        copies[at].wait()
    gain = gain_ref[...]
    inverse, scaled, _ = normalise(x_ref[order_ref[direction, 0, 1]], gain)
    grad_ref[0] = own[...]
    grad_ref[1], grad_gain = input_gradient(gproj_ref[...], qkv_ref[...], gain, scaled, inverse, up_ref[...])
    gain_out[...] = gain1[...] + grad_gain
    written = pltpu.make_async_copy(grad_ref, grads_hbm.at[direction], sems.at[6])
    written.start()
    written.wait()


def backward_pass(direction, order, act, gain, qkv, out, seed, forward, gain1, moved, own, grads=None, after=()):
    seq, model = act.shape[1:]
    width = qkv.shape[1]
    query_width = out.shape[0]
    hbm, vmem = pltpu.HBM, pltpu.VMEM
    _, project, attended, soft = forward
    inputs = [(a, hbm) for a in (order, act, qkv, out, gain, seed)]
    inputs += [(a, vmem) for a in (project, attended, soft, gain1, moved, own)]
    aliases = {}
    if grads is not None:
        aliases = {len(inputs): 3}
        inputs += [(grads, hbm)]
    return call(
        functools.partial(backward_kernel, direction=direction, kept=len(aliases)),
        "backward_pass",
        inputs,
        [
            ((seq, model), BF16, vmem),
            ((seq, width), BF16, vmem),
            ((1, model), F32, vmem),
            ((2, 2, seq, model), BF16, hbm),
        ],
        [
            pltpu.SMEM(order.shape, jnp.int32),
            pltpu.VMEM(act.shape, BF16),
            pltpu.VMEM((model, width), BF16),
            pltpu.VMEM((query_width, model), BF16),
            pltpu.VMEM((1, model), F32),
            pltpu.VMEM((2, seq, model), BF16),
            pltpu.SemaphoreType.DMA((7,)),
        ],
        after,
        aliases,
    )


def cut(rows, pieces):
    return max(p for p in range(1, pieces + 1) if rows % (16 * p) == 0)


def hand_out(blocks, sends, keep_ref):
    parts = blocks.shape[0]
    replica = lax.axis_index("dp")
    for k in range(parts - 1):
        at = lax.rem(replica + 1 + k, parts)
        for p, ref in enumerate(sends):
            rows = ref.shape[1]
            ref[k] = blocks[at, p * rows : (p + 1) * rows, :]
    keep_ref[...] = blocks[replica]


def outproj_kernel(up_hbm, seed_hbm, att1, att2, moved, *refs, direction):
    *sends, keep_ref, up1_ref, up2_ref, blocks, sems = refs
    copy = pltpu.make_async_copy(up_hbm, up1_ref, sems.at[0])
    copy.start()
    choose_upstream(direction, moved, seed_hbm, up2_ref, sems.at[1])
    parts, rows, _ = blocks.shape
    copy.wait()
    total = dot(att1[...], up1_ref[...], TN) + dot(att2[...], up2_ref[...], TN)
    for q in range(parts):
        blocks[q] = total[q * rows : (q + 1) * rows].astype(BF16)
    hand_out(blocks, sends, keep_ref)


def outproj_pass(direction, att1, att2, upstream, moved, seed, parts, after=()):
    seq, model = moved.shape
    rows = att1.shape[1] // parts
    pieces = cut(rows, PIECES_OUT)
    hbm, vmem = pltpu.HBM, pltpu.VMEM
    *sends, keep = call(
        functools.partial(outproj_kernel, direction=direction),
        "outproj_pass",
        [(upstream, hbm), (seed, hbm), (att1, vmem), (att2, vmem), (moved, vmem)],
        [((parts - 1, rows // pieces, model), BF16, vmem)] * pieces + [((rows, model), BF16, vmem)],
        [
            pltpu.VMEM((seq, model), BF16),
            pltpu.VMEM((seq, model), BF16),
            pltpu.VMEM((parts, rows, model), BF16),
            pltpu.SemaphoreType.DMA((2,)),
        ],
        after,
    )
    return sends, keep


def qkv_kernel(normed1, gproj1, normed2, gproj2, gain, *refs):
    *sends, keep_ref, blocks = refs
    parts, height, width = blocks.shape
    rows = normed1.shape[1] // parts
    for q in range(parts):
        at = slice(q * rows, (q + 1) * rows)
        total = dot(normed1[:, at], gproj1[...], TN) + dot(normed2[:, at], gproj2[...], TN)
        blocks[q, :rows, :] = total.astype(BF16)
        blocks[q, rows:, :] = jnp.zeros((height - rows, width), BF16)
        blocks[q, rows:, :rows] = jnp.broadcast_to(gain[:, at], (height - rows, rows)).astype(BF16)
    hand_out(blocks, sends, keep_ref)


def qkv_pass(normed1, gproj1, normed2, gproj2, gain, parts, after=()):
    rows, width = normed1.shape[1] // parts + PAD, gproj1.shape[1]
    pieces = cut(rows, PIECES_QKV)
    vmem = pltpu.VMEM
    *sends, keep = call(
        qkv_kernel,
        "qkv_pass",
        [(a, vmem) for a in (normed1, gproj1, normed2, gproj2, gain)],
        [((parts - 1, rows // pieces, width), BF16, vmem)] * pieces + [((rows, width), BF16, vmem)],
        [pltpu.VMEM((parts, rows, width), BF16)],
        after,
    )
    return sends, keep


def layout(parts, query_width, model, width):
    unit = math.gcd(model, width)
    out_rows, qkv_rows = query_width // parts, model // parts
    start = out_rows * (model // unit)
    gain_at = start + qkv_rows * (width // unit)
    return unit, out_rows, qkv_rows, start, gain_at, gain_at + PACKED_PAD


def packed_kernel(normed1, gproj1, att1, up1_hbm, normed2, gproj2, att2, up2, gain, *refs):
    *sends, keep_ref, blocks, up1, sem = refs
    copy = pltpu.make_async_copy(up1_hbm, up1, sem)
    copy.start()
    parts = blocks.shape[0]
    model, width = normed1.shape[1], gproj1.shape[1]
    unit, out_rows, qkv_rows, start, gain_at, _ = layout(parts, att1.shape[1], model, width)
    row = lax.broadcasted_iota(jnp.int32, (PACKED_PAD, unit), 0)
    for q in range(parts):
        at = slice(q * qkv_rows, (q + 1) * qkv_rows)
        qkv = dot(normed1[:, at], gproj1[...], TN) + dot(normed2[:, at], gproj2[...], TN)
        for c in range(width // unit):
            first = start + c * qkv_rows
            blocks[q, first : first + qkv_rows, :] = qkv[:, c * unit : (c + 1) * unit].astype(BF16)
        lines = jnp.zeros((PACKED_PAD, unit), F32)
        for i in range(pl.cdiv(qkv_rows, unit)):
            line = gain[:, q * qkv_rows + i * unit : q * qkv_rows + min((i + 1) * unit, qkv_rows)]
            if line.shape[1] < unit:
                line = jnp.concatenate([line, jnp.zeros((1, unit - line.shape[1]), F32)], axis=1)
            lines = jnp.where(row == i, line, lines)
        blocks[q, gain_at:, :] = lines.astype(BF16)
    copy.wait()
    out = dot(att1[...], up1[...], TN) + dot(att2[...], up2[...], TN)
    for q in range(parts):
        for c in range(model // unit):
            blocks[q, c * out_rows : (c + 1) * out_rows, :] = out[
                q * out_rows : (q + 1) * out_rows, c * unit : (c + 1) * unit
            ].astype(BF16)
    hand_out(blocks, sends, keep_ref)


def packed_pass(normed1, gproj1, att1, up1, normed2, gproj2, att2, up2, gain, parts, after=()):
    seq, model = normed1.shape
    unit, _, _, _, _, rows = layout(parts, att1.shape[1], model, gproj1.shape[1])
    pieces = cut(rows, PIECES)
    hbm, vmem = pltpu.HBM, pltpu.VMEM
    *sends, keep = call(
        packed_kernel,
        "packed_pass",
        [(normed1, vmem), (gproj1, vmem), (att1, vmem), (up1, hbm)]
        + [(a, vmem) for a in (normed2, gproj2, att2, up2, gain)],
        [((parts - 1, rows // pieces, unit), BF16, vmem)] * pieces + [((rows, unit), BF16, vmem)],
        [
            pltpu.VMEM((parts, rows, unit), BF16),
            pltpu.VMEM((seq, model), BF16),
            pltpu.SemaphoreType.DMA(()),
        ],
        after,
    )
    return sends, keep


def final_kernel(keep, outer_out, inner_out, mirror_qkv, *refs, parts, pieces):
    moved, refs = refs[: (parts - 1) * pieces], refs[(parts - 1) * pieces :]
    gain_hbm, qkv_hbm, out_hbm, gain_ref, qkv_ref, out_ref, sems = refs
    model, width = out_ref.shape[1], qkv_ref.shape[1]
    unit, out_rows, qkv_rows, start, gain_at, rows = layout(parts, out_ref.shape[0] * parts, model, width)
    each = rows // pieces

    def total(first, count):
        result = keep[first : first + count, :].astype(F32)
        for k in range(parts - 1):
            taken, at = [], first
            while at < first + count:
                p = at // each
                until = min(first + count, (p + 1) * each)
                taken.append(moved[k * pieces + p][at - p * each : until - p * each, :].astype(F32))
                at = until
            result = result + (taken[0] if len(taken) == 1 else jnp.concatenate(taken, axis=0))
        return result

    for c in range(width // unit):
        columns = slice(c * unit, (c + 1) * unit)
        qkv_ref[:, columns] = total(start + c * qkv_rows, qkv_rows) + mirror_qkv[:qkv_rows, columns].astype(F32)
    copies = [pltpu.make_async_copy(qkv_ref, qkv_hbm, sems.at[0])]
    copies[0].start()
    for c in range(model // unit):
        columns = slice(c * unit, (c + 1) * unit)
        out_ref[:, columns] = total(c * out_rows, out_rows) + (outer_out[:, columns] + inner_out[:, columns]).astype(F32)
    copies.append(pltpu.make_async_copy(out_ref, out_hbm, sems.at[1]))
    copies[1].start()
    lines = total(gain_at, PACKED_PAD)
    other = mirror_qkv[qkv_rows:, :].astype(F32)
    for i in range(pl.cdiv(qkv_rows, unit)):
        until = min((i + 1) * unit, qkv_rows)
        gain_ref[:, i * unit : until] = lines[i : i + 1, : until - i * unit] + other[:1, i * unit : until]
    copies.append(pltpu.make_async_copy(gain_ref, gain_hbm, sems.at[2]))
    copies[2].start()
    for copy in copies:
        copy.wait()


def final_pass(keep, outer_out, inner_out, mirror_qkv, moved, parts, query_width, model, width):
    hbm, vmem = pltpu.HBM, pltpu.VMEM
    shapes = ((1, model // parts), (model // parts, width), (query_width // parts, model))
    return call(
        functools.partial(final_kernel, parts=parts, pieces=len(moved[0])),
        "final_pass",
        [(keep, vmem), (outer_out, vmem), (inner_out, vmem), (mirror_qkv, vmem)] + [(m, vmem) for per in moved for m in per],
        [(shape, F32, hbm) for shape in shapes],
        [pltpu.VMEM(shape, F32) for shape in shapes] + [pltpu.SemaphoreType.DMA((3,))],
    )


def sum_kernel(keep, *refs):
    *moved, sum_ref = refs
    pieces = len(moved)
    at = 0
    for p in range(pieces):
        rows = moved[p].shape[1]
        total = keep[at : at + rows, :].astype(F32)
        for k in range(moved[p].shape[0]):
            total = total + moved[p][k].astype(F32)
        sum_ref[at : at + rows, :] = total.astype(BF16)
        at += rows


def sum_pass(keep, moved, after=()):
    vmem = pltpu.VMEM
    pieces = [jnp.stack([per[p] for per in moved]) if len(moved) > 1 else moved[0][p][None] for p in range(len(moved[0]))]
    (total,) = call(
        sum_kernel, "sum_pass", [(keep, vmem)] + [(p, vmem) for p in pieces], [(keep.shape, BF16, vmem)], [], after
    )
    return total


def shifted(value, axis, steps):
    count = lax.axis_size(axis)
    first, last = (max(0, -steps), min(count, count - steps))
    return lax.ppermute(value, axis, [(source, source + steps) for source in range(first, last)])


def mirrored(value, axis, sections=None):
    count = lax.axis_size(axis)
    return lax.ppermute(value, axis, [(i, count - 1 - i) for i in (range(count) if sections is None else sections)])


def exchanged(sends, axis):
    parts = lax.axis_size(axis)
    return [
        [lax.ppermute(send[k], axis, [(i, (i + 1 + k) % parts) for i in range(parts)]) for send in sends]
        for k in range(parts - 1)
    ]


def shards(
    act_down, act_up, grad_down, grad_up, seed_down, seed_up, gain_down, qkv_down, outproj_down,
    gain_up, qkv_up, outproj_up, doc_offsets, slot_order,
):
    parts = lax.axis_size("dp")
    query_width, model = outproj_down.shape[1:]
    width = qkv_down.shape[2]
    ints = (slot_order, doc_offsets.reshape(slot_order.shape))
    down = (gain_down, qkv_down[0], outproj_down[0])
    up = (gain_up, qkv_up[0], outproj_up[0])

    sections = lax.axis_size("section")
    edge = sections // 4
    outer = [*range(edge), *range(sections - edge, sections)]
    inner = range(edge, sections - edge)

    up_one = first_pass(1, ints, act_up[0], *up, grad_up[0], limit=FIRST_LIMIT)
    up_moved = shifted(up_one[0], "section", 1)
    down_one = first_pass(0, ints, act_down[0], *down, grad_down[0], limit=60 * 1024 * 1024, after=(up_one[4],))
    down_moved = shifted(down_one[0], "section", -1)
    up_forward = forward_pass(1, ints, act_up[0], gain_up, qkv_up[0], query_width, after=(down_one[3],))
    sends, keep = outproj_pass(1, up_one[2], up_forward[2], grad_up[0], up_moved, seed_up, parts)
    up_out = sum_pass(keep, exchanged(sends, "dp"))
    outer_out = mirrored(up_out, "section", outer)
    inner_out = mirrored(up_out, "section", inner)
    up_two = backward_pass(
        1, slot_order, act_up[0], *up, seed_up, up_forward, up_one[4], up_moved, up_one[0], after=(up_out,)
    )
    sends, keep = qkv_pass(up_one[1], up_one[3], up_forward[0], up_two[1], up_two[2], parts, after=(down_moved,))
    down_forward = forward_pass(0, ints, act_down[0], gain_down, qkv_down[0], query_width, after=(keep,))
    up_qkv = sum_pass(keep, exchanged(sends, "dp"), after=(outer_out, down_forward[2]))
    mirror_qkv = mirrored(up_qkv, "section")
    down_two = backward_pass(
        0, slot_order, act_down[0], *down, seed_down, down_forward, down_one[4], down_moved, down_one[0],
        grads=up_two[3], after=(up_qkv, inner_out),
    )
    sends, keep = packed_pass(
        down_one[1], down_one[3], down_one[2], grad_down[0],
        down_forward[0], down_two[1], down_forward[2], down_two[0], down_two[2], parts,
    )
    grad_gain, grad_qkv, grad_outproj = final_pass(
        keep, outer_out, inner_out, mirror_qkv, exchanged(sends, "dp"), parts, query_width, model, width
    )
    return (down_two[3][:, None], grad_gain, grad_qkv[None], grad_outproj[None])


def solution(mesh):
    return jax.shard_map(
        shards,
        mesh=mesh,
        in_specs=(
            P("section", None, "dp", None),
            P("section", None, "dp", None),
            P("section", "dp", None),
            P("section", "dp", None),
            P("dp", None),
            P("dp", None),
            P("section", None),
            P("section", None, None),
            P("section", None, None),
            P("section", None),
            P("section", None, None),
            P("section", None, None),
            P(None, "section", None, "dp"),
            P(None, "section", None),
        ),
        out_specs=(
            P(None, "section", None, "dp", None),
            P("section", "dp"),
            P("section", "dp", None),
            P("section", "dp", None),
        ),
        check_vma=False,
    )
```

```python
import functools
import math
import jax
import jax.numpy as jnp
from jax import lax
from jax.experimental import pallas as pl
from jax.experimental.pallas import tpu as pltpu
from jax.sharding import PartitionSpec as P

HEADS = 8
KV_HEADS = 2
EPSILON = 1e-05
MASKED = -1e30
PAD = 16
LANES = 128
PACKED_PAD = 32
PIECES = 2
PIECES_OUT = 2
PIECES_QKV = 3
VMEM_LIMIT = 24 * 1024 * 1024
FIRST_LIMIT = 60 * 1024 * 1024
F32 = jnp.float32
BF16 = jnp.bfloat16
NN = (((1,), (0,)), ((), ()))
NT = (((1,), (1,)), ((), ()))
TN = (((0,), (0,)), ((), ()))


def dot(a, b, dims=NN):
    return lax.dot_general(a, b, dims, preferred_element_type=F32)


def doubled(pair, half):
    wide = pair.astype(F32)
    turned = pltpu.roll(wide, half, 1)
    left = lax.broadcasted_iota(jnp.int32, wide.shape, 1) < half
    zero = jnp.zeros_like(wide)
    out = []
    for g in range(KV_HEADS):
        a, b = (wide, turned) if g == 0 else (turned, wide)
        out.append(
            jnp.concatenate([jnp.where(left, a, zero), jnp.where(left, zero, b)], axis=0).astype(BF16)
        )
    return out


def mask_bias(seq, offset):
    row = lax.broadcasted_iota(jnp.int32, (seq, seq), 0)
    col = lax.broadcasted_iota(jnp.int32, (seq, seq), 1)
    start = jnp.where(row >= offset, offset, 0)
    return jnp.where((col <= row) & (col >= start), 0.0, MASKED).astype(F32)


def normalise(x, gain):
    xf = x.astype(F32)
    inverse = lax.rsqrt(jnp.mean(xf * xf, axis=1, keepdims=True) + EPSILON)
    scaled = xf * inverse
    return inverse, scaled, (scaled * gain).astype(BF16)


def softmax(scores):
    e = jnp.exp(scores - jnp.max(scores, axis=1, keepdims=True))
    return (e * (1.0 / jnp.sum(e, axis=1, keepdims=True))).astype(BF16)


def pair_columns(array, query_width):
    wide = 2 * (query_width // HEADS)
    return [array[:, p * wide : (p + 1) * wide] for p in range(HEADS // 2)]


def forward_heads(project, offset, query_width, soft_ref):
    seq = project.shape[0]
    half = query_width // HEADS
    wide = 2 * half
    keys = doubled(project[:, query_width : query_width + wide], half)
    values = doubled(project[:, query_width + wide :], half)
    bias = mask_bias(seq, offset)
    scale = jnp.asarray(half ** (-0.5), BF16)
    pairs = HEADS // 2
    group = [p * KV_HEADS // pairs for p in range(pairs)]
    queries = pair_columns(project, query_width)
    scores = [dot(queries[p] * scale, keys[group[p]], NT) for p in range(pairs)]
    for p in range(pairs):
        for t in range(2):
            at = slice(t * seq, (t + 1) * seq)
            soft_ref[p, :, at] = softmax(scores[p][:, at] + bias)
    return [dot(soft_ref[p], values[group[p]]) for p in range(pairs)]


def backward_heads(project, attended, grad_attended, query_width, soft_ref):
    seq = project.shape[0]
    half = query_width // HEADS
    wide = 2 * half
    keys = doubled(project[:, query_width : query_width + wide], half)
    values = doubled(project[:, query_width + wide :], half)
    scale = half ** (-0.5)
    pairs = HEADS // 2
    group = [p * KV_HEADS // pairs for p in range(pairs)]
    left = lax.broadcasted_iota(jnp.int32, (seq, wide), 1) < half
    queries = [q * jnp.asarray(scale, BF16) for q in pair_columns(project, query_width)]
    grads = pair_columns(grad_attended, query_width)
    grad_soft = [dot(grads[p], values[group[p]], NT) for p in range(pairs)]
    values_parts = [dot(grads[p], soft_ref[p], TN) for p in range(pairs)]
    grad_scores = []
    for p in range(pairs):
        both = attended[p].astype(F32) * grads[p].astype(F32)
        rows = [
            jnp.sum(jnp.where(left, both, 0.0), axis=1, keepdims=True),
            jnp.sum(jnp.where(left, 0.0, both), axis=1, keepdims=True),
        ]
        columns = [slice(t * seq, (t + 1) * seq) for t in range(2)]
        grad_scores.append(
            jnp.concatenate(
                [
                    (soft_ref[p, :, at].astype(F32) * (grad_soft[p][:, at] - row)).astype(BF16)
                    for at, row in zip(columns, rows)
                ],
                axis=1,
            )
        )
    grad_queries = [dot(grad_scores[p], keys[group[p]]) * scale for p in range(pairs)]
    keys_parts = [dot(queries[p], grad_scores[p], TN) for p in range(pairs)]

    def joined(parts):
        sums = []
        for g in range(KV_HEADS):
            part = sum(parts[p] for p in range(pairs) if group[p] == g)
            sums.append(part[:half, :seq] + part[half:, seq:])
        return jnp.concatenate(sums, axis=0).T

    columns = [*grad_queries, joined(keys_parts), joined(values_parts)]
    return jnp.concatenate([c.astype(BF16) for c in columns], axis=1)


def input_gradient(grad_project, qkv, gain, scaled, inverse, upstream):
    grad_normed = dot(grad_project, qkv, NT)
    grad_hat = grad_normed * gain
    part = grad_normed * scaled
    grad_gain = jnp.sum(part, axis=0, keepdims=True)
    mean = jnp.mean(part * gain, axis=1, keepdims=True)
    grad_in = upstream.astype(F32) + inverse * (grad_hat - scaled * mean)
    return grad_in.astype(BF16), grad_gain


def whole(memory=pltpu.VMEM):
    return pl.BlockSpec(memory_space=memory)


def call(kernel, name, inputs, outputs, scratch, after=(), aliases=None, limit=VMEM_LIMIT):
    count = len(inputs)

    def ordered(*refs):
        kernel(*refs[:count], *refs[count + len(after) :])

    return pl.pallas_call(
        ordered,
        out_shape=tuple(jax.ShapeDtypeStruct(shape, dtype) for shape, dtype, _ in outputs),
        in_specs=[whole(space) for _, space in inputs] + [whole(pl.ANY)] * len(after),
        out_specs=tuple(whole(space) for _, _, space in outputs),
        scratch_shapes=scratch,
        input_output_aliases=aliases or {},
        compiler_params=pltpu.CompilerParams(vmem_limit_bytes=limit),
        cost_estimate=pl.CostEstimate(flops=1, bytes_accessed=1, transcendentals=0),
        name=name,
    )(*(array for array, _ in inputs), *after)


def start_all(sources, targets, sems):
    copies = [pltpu.make_async_copy(a, b, sems.at[i]) for i, (a, b) in enumerate(zip(sources, targets))]
    for copy in copies:
        copy.start()
    return copies


def first_kernel(order, offsets, act, qkv_hbm, out_hbm, up_hbm, gain_hbm, *refs, direction):
    grad_ref, normed_ref, attended_ref, project_ref, gain_out = refs[:5]
    order_ref, offsets_ref, x_ref, qkv_ref, out_ref, up_ref, gain_ref, soft_ref, sems = refs[5:]
    sources = (order, offsets, gain_hbm, act, qkv_hbm, up_hbm, out_hbm)
    targets = (order_ref, offsets_ref, gain_ref, x_ref, qkv_ref, up_ref, out_ref)
    copies = [pltpu.make_async_copy(a, b, sems.at[i]) for i, (a, b) in enumerate(zip(sources, targets))]
    for copy in copies[:5]:
        copy.start()
    query_width = out_hbm.shape[0]
    for copy in copies[:4]:
        copy.wait()
    for copy in copies[5:]:
        copy.start()
    which = order_ref[direction, 0, 0]
    offset = offsets_ref[direction, 0, which]
    gain = gain_ref[...]
    _, _, normed = normalise(x_ref[which], gain)
    normed_ref[...] = normed
    copies[4].wait()
    project = dot(normed, qkv_ref[...]).astype(BF16)
    attended = forward_heads(project, offset, query_width, soft_ref)
    attended_ref[...] = jnp.concatenate([a.astype(BF16) for a in attended], axis=1)
    copies[5].wait()
    copies[6].wait()
    grad_attended = dot(up_ref[...], out_ref[...], NT).astype(BF16)
    grad_project = backward_heads(project, attended, grad_attended, query_width, soft_ref)
    project_ref[...] = grad_project
    inverse, scaled, _ = normalise(x_ref[which], gain)
    grad_ref[...], gain_out[...] = input_gradient(grad_project, qkv_ref[...], gain, scaled, inverse, up_ref[...])


def first_pass(direction, ints, act, gain, qkv, out, upstream, after=(), limit=VMEM_LIMIT):
    seq, model = act.shape[1:]
    width = qkv.shape[1]
    query_width = out.shape[0]
    hbm, vmem = pltpu.HBM, pltpu.VMEM
    return call(
        functools.partial(first_kernel, direction=direction),
        "first_pass",
        [(a, hbm) for a in (*ints, act, qkv, out, upstream, gain)],
        [
            ((seq, model), BF16, vmem),
            ((seq, model), BF16, vmem),
            ((seq, query_width), BF16, vmem),
            ((seq, width), BF16, vmem),
            ((1, model), F32, vmem),
        ],
        [pltpu.SMEM(a.shape, jnp.int32) for a in ints]
        + [
            pltpu.VMEM(act.shape, BF16),
            pltpu.VMEM((model, width), BF16),
            pltpu.VMEM((query_width, model), BF16),
            pltpu.VMEM((seq, model), BF16),
            pltpu.VMEM((1, model), F32),
            pltpu.VMEM((HEADS // 2, seq, 2 * seq), BF16),
            pltpu.SemaphoreType.DMA((7,)),
        ],
        after,
        limit=limit,
    )


def forward_kernel(order, offsets, act, qkv_hbm, gain_hbm, *refs, direction, query_width):
    normed_ref, project_ref, attended_ref, soft_ref = refs[:4]
    order_ref, offsets_ref, x_ref, qkv_ref, gain_ref, sems = refs[4:]
    copies = start_all(
        (order, offsets, act, gain_hbm, qkv_hbm), (order_ref, offsets_ref, x_ref, gain_ref, qkv_ref), sems
    )
    for copy in copies[:4]:
        copy.wait()
    which = order_ref[direction, 0, 1]
    offset = offsets_ref[direction, 0, which]
    _, _, normed = normalise(x_ref[which], gain_ref[...])
    normed_ref[...] = normed
    copies[4].wait()
    project = dot(normed, qkv_ref[...]).astype(BF16)
    project_ref[...] = project
    attended = forward_heads(project, offset, query_width, soft_ref)
    attended_ref[...] = jnp.concatenate([a.astype(BF16) for a in attended], axis=1)


def forward_pass(direction, ints, act, gain, qkv, query_width, after=()):
    seq, model = act.shape[1:]
    width = qkv.shape[1]
    hbm, vmem = pltpu.HBM, pltpu.VMEM
    return call(
        functools.partial(forward_kernel, direction=direction, query_width=query_width),
        "forward_pass",
        [(a, hbm) for a in (*ints, act, qkv, gain)],
        [
            ((seq, model), BF16, vmem),
            ((seq, width), BF16, vmem),
            ((seq, query_width), BF16, vmem),
            ((HEADS // 2, seq, 2 * seq), BF16, vmem),
        ],
        [pltpu.SMEM(a.shape, jnp.int32) for a in ints]
        + [
            pltpu.VMEM(act.shape, BF16),
            pltpu.VMEM((model, width), BF16),
            pltpu.VMEM((1, model), F32),
            pltpu.SemaphoreType.DMA((5,)),
        ],
        after,
    )


def choose_upstream(direction, moved, seed_hbm, up_ref, sem):
    seeded = lax.axis_index("section") == (lax.axis_size("section") - 1 if direction == 0 else 0)

    @pl.when(seeded)
    def _():
        copy = pltpu.make_async_copy(seed_hbm, up_ref, sem)
        copy.start()
        copy.wait()

    @pl.when(jnp.logical_not(seeded))
    def _():
        up_ref[...] = moved[...]


def backward_kernel(
    order, act, qkv_hbm, out_hbm, gain_hbm, seed_hbm, project_ref, attended_ref, soft_ref, gain1, moved, own,
    *refs, direction, kept,
):
    up_ref, gproj_ref, gain_out, grads_hbm = refs[kept : kept + 4]
    order_ref, x_ref, qkv_ref, out_ref, gain_ref, grad_ref, sems = refs[kept + 4 :]
    copies = start_all(
        (order, act, gain_hbm, out_hbm, qkv_hbm), (order_ref, x_ref, gain_ref, out_ref, qkv_ref), sems
    )
    choose_upstream(direction, moved, seed_hbm, up_ref, sems.at[5])
    copies[3].wait()
    query_width = out_ref.shape[0]
    wide = 2 * query_width // HEADS
    grad_attended = dot(up_ref[...], out_ref[...], NT).astype(BF16)
    attended = [attended_ref[:, p * wide : (p + 1) * wide] for p in range(HEADS // 2)]
    gproj_ref[...] = backward_heads(project_ref[...], attended, grad_attended, query_width, soft_ref)
    for at in (0, 1, 2, 4):
        copies[at].wait()
    gain = gain_ref[...]
    inverse, scaled, _ = normalise(x_ref[order_ref[direction, 0, 1]], gain)
    grad_ref[0] = own[...]
    grad_ref[1], grad_gain = input_gradient(gproj_ref[...], qkv_ref[...], gain, scaled, inverse, up_ref[...])
    gain_out[...] = gain1[...] + grad_gain
    written = pltpu.make_async_copy(grad_ref, grads_hbm.at[direction], sems.at[6])
    written.start()
    written.wait()


def backward_pass(direction, order, act, gain, qkv, out, seed, forward, gain1, moved, own, grads=None, after=()):
    seq, model = act.shape[1:]
    width = qkv.shape[1]
    query_width = out.shape[0]
    hbm, vmem = pltpu.HBM, pltpu.VMEM
    _, project, attended, soft = forward
    inputs = [(a, hbm) for a in (order, act, qkv, out, gain, seed)]
    inputs += [(a, vmem) for a in (project, attended, soft, gain1, moved, own)]
    aliases = {}
    if grads is not None:
        aliases = {len(inputs): 3}
        inputs += [(grads, hbm)]
    return call(
        functools.partial(backward_kernel, direction=direction, kept=len(aliases)),
        "backward_pass",
        inputs,
        [
            ((seq, model), BF16, vmem),
            ((seq, width), BF16, vmem),
            ((1, model), F32, vmem),
            ((2, 2, seq, model), BF16, hbm),
        ],
        [
            pltpu.SMEM(order.shape, jnp.int32),
            pltpu.VMEM(act.shape, BF16),
            pltpu.VMEM((model, width), BF16),
            pltpu.VMEM((query_width, model), BF16),
            pltpu.VMEM((1, model), F32),
            pltpu.VMEM((2, seq, model), BF16),
            pltpu.SemaphoreType.DMA((7,)),
        ],
        after,
        aliases,
    )


def cut(rows, pieces):
    return max(p for p in range(1, pieces + 1) if rows % (16 * p) == 0)


def hand_out(blocks, sends, keep_ref):
    parts = blocks.shape[0]
    replica = lax.axis_index("dp")
    for k in range(parts - 1):
        at = lax.rem(replica + 1 + k, parts)
        for p, ref in enumerate(sends):
            rows = ref.shape[1]
            ref[k] = blocks[at, p * rows : (p + 1) * rows, :]
    keep_ref[...] = blocks[replica]


def outproj_kernel(up_hbm, seed_hbm, att1, att2, moved, *refs, direction):
    *sends, keep_ref, up1_ref, up2_ref, blocks, sems = refs
    copy = pltpu.make_async_copy(up_hbm, up1_ref, sems.at[0])
    copy.start()
    choose_upstream(direction, moved, seed_hbm, up2_ref, sems.at[1])
    parts, rows, _ = blocks.shape
    copy.wait()
    total = dot(att1[...], up1_ref[...], TN) + dot(att2[...], up2_ref[...], TN)
    for q in range(parts):
        blocks[q] = total[q * rows : (q + 1) * rows].astype(BF16)
    hand_out(blocks, sends, keep_ref)


def outproj_pass(direction, att1, att2, upstream, moved, seed, parts, after=()):
    seq, model = moved.shape
    rows = att1.shape[1] // parts
    pieces = cut(rows, PIECES_OUT)
    hbm, vmem = pltpu.HBM, pltpu.VMEM
    *sends, keep = call(
        functools.partial(outproj_kernel, direction=direction),
        "outproj_pass",
        [(upstream, hbm), (seed, hbm), (att1, vmem), (att2, vmem), (moved, vmem)],
        [((parts - 1, rows // pieces, model), BF16, vmem)] * pieces + [((rows, model), BF16, vmem)],
        [
            pltpu.VMEM((seq, model), BF16),
            pltpu.VMEM((seq, model), BF16),
            pltpu.VMEM((parts, rows, model), BF16),
            pltpu.SemaphoreType.DMA((2,)),
        ],
        after,
    )
    return sends, keep


def qkv_kernel(normed1, gproj1, normed2, gproj2, gain, *refs):
    *sends, keep_ref, blocks = refs
    parts, height, width = blocks.shape
    rows = normed1.shape[1] // parts
    for q in range(parts):
        at = slice(q * rows, (q + 1) * rows)
        total = dot(normed1[:, at], gproj1[...], TN) + dot(normed2[:, at], gproj2[...], TN)
        blocks[q, :rows, :] = total.astype(BF16)
        blocks[q, rows:, :] = jnp.zeros((height - rows, width), BF16)
        blocks[q, rows:, :rows] = jnp.broadcast_to(gain[:, at], (height - rows, rows)).astype(BF16)
    hand_out(blocks, sends, keep_ref)


def qkv_pass(normed1, gproj1, normed2, gproj2, gain, parts, after=()):
    rows, width = normed1.shape[1] // parts + PAD, gproj1.shape[1]
    pieces = cut(rows, PIECES_QKV)
    vmem = pltpu.VMEM
    *sends, keep = call(
        qkv_kernel,
        "qkv_pass",
        [(a, vmem) for a in (normed1, gproj1, normed2, gproj2, gain)],
        [((parts - 1, rows // pieces, width), BF16, vmem)] * pieces + [((rows, width), BF16, vmem)],
        [pltpu.VMEM((parts, rows, width), BF16)],
        after,
    )
    return sends, keep


def layout(parts, query_width, model, width):
    unit = math.gcd(model, width)
    out_rows, qkv_rows = query_width // parts, model // parts
    start = out_rows * (model // unit)
    gain_at = start + qkv_rows * (width // unit)
    return unit, out_rows, qkv_rows, start, gain_at, gain_at + PACKED_PAD


def packed_kernel(normed1, gproj1, att1, up1_hbm, normed2, gproj2, att2, up2, gain, *refs):
    *sends, keep_ref, blocks, up1, sem = refs
    copy = pltpu.make_async_copy(up1_hbm, up1, sem)
    copy.start()
    parts = blocks.shape[0]
    model, width = normed1.shape[1], gproj1.shape[1]
    unit, out_rows, qkv_rows, start, gain_at, _ = layout(parts, att1.shape[1], model, width)
    row = lax.broadcasted_iota(jnp.int32, (PACKED_PAD, unit), 0)
    for q in range(parts):
        at = slice(q * qkv_rows, (q + 1) * qkv_rows)
        qkv = dot(normed1[:, at], gproj1[...], TN) + dot(normed2[:, at], gproj2[...], TN)
        for c in range(width // unit):
            first = start + c * qkv_rows
            blocks[q, first : first + qkv_rows, :] = qkv[:, c * unit : (c + 1) * unit].astype(BF16)
        lines = jnp.zeros((PACKED_PAD, unit), F32)
        for i in range(pl.cdiv(qkv_rows, unit)):
            line = gain[:, q * qkv_rows + i * unit : q * qkv_rows + min((i + 1) * unit, qkv_rows)]
            if line.shape[1] < unit:
                line = jnp.concatenate([line, jnp.zeros((1, unit - line.shape[1]), F32)], axis=1)
            lines = jnp.where(row == i, line, lines)
        blocks[q, gain_at:, :] = lines.astype(BF16)
    copy.wait()
    out = dot(att1[...], up1[...], TN) + dot(att2[...], up2[...], TN)
    for q in range(parts):
        for c in range(model // unit):
            blocks[q, c * out_rows : (c + 1) * out_rows, :] = out[
                q * out_rows : (q + 1) * out_rows, c * unit : (c + 1) * unit
            ].astype(BF16)
    hand_out(blocks, sends, keep_ref)


def packed_pass(normed1, gproj1, att1, up1, normed2, gproj2, att2, up2, gain, parts, after=()):
    seq, model = normed1.shape
    unit, _, _, _, _, rows = layout(parts, att1.shape[1], model, gproj1.shape[1])
    pieces = cut(rows, PIECES)
    hbm, vmem = pltpu.HBM, pltpu.VMEM
    *sends, keep = call(
        packed_kernel,
        "packed_pass",
        [(normed1, vmem), (gproj1, vmem), (att1, vmem), (up1, hbm)]
        + [(a, vmem) for a in (normed2, gproj2, att2, up2, gain)],
        [((parts - 1, rows // pieces, unit), BF16, vmem)] * pieces + [((rows, unit), BF16, vmem)],
        [
            pltpu.VMEM((parts, rows, unit), BF16),
            pltpu.VMEM((seq, model), BF16),
            pltpu.SemaphoreType.DMA(()),
        ],
        after,
    )
    return sends, keep


def own_kernel(keep, outer_out, inner_out, *refs, parts, pieces):
    moved, refs = refs[: (parts - 1) * pieces], refs[(parts - 1) * pieces :]
    out_hbm, qkv_ref, gain_ref, out_ref, sem = refs
    model, width = out_ref.shape[1], qkv_ref.shape[1]
    unit, out_rows, qkv_rows, start, gain_at, rows = layout(parts, out_ref.shape[0] * parts, model, width)
    each = rows // pieces

    def total(first, count):
        result = keep[first : first + count, :].astype(F32)
        for k in range(parts - 1):
            taken, at = [], first
            while at < first + count:
                p = at // each
                until = min(first + count, (p + 1) * each)
                taken.append(moved[k * pieces + p][at - p * each : until - p * each, :].astype(F32))
                at = until
            result = result + (taken[0] if len(taken) == 1 else jnp.concatenate(taken, axis=0))
        return result

    for c in range(model // unit):
        columns = slice(c * unit, (c + 1) * unit)
        out_ref[:, columns] = total(c * out_rows, out_rows) + (outer_out[:, columns] + inner_out[:, columns]).astype(F32)
    copy = pltpu.make_async_copy(out_ref, out_hbm, sem)
    copy.start()
    for c in range(width // unit):
        qkv_ref[:, c * unit : (c + 1) * unit] = total(start + c * qkv_rows, qkv_rows)
    lines = total(gain_at, PACKED_PAD)
    for i in range(pl.cdiv(qkv_rows, unit)):
        until = min((i + 1) * unit, qkv_rows)
        gain_ref[:, i * unit : until] = lines[i : i + 1, : until - i * unit]
    copy.wait()


def own_pass(keep, outer_out, inner_out, moved, parts, query_width, model, width):
    hbm, vmem = pltpu.HBM, pltpu.VMEM
    out_shape = (query_width // parts, model)
    return call(
        functools.partial(own_kernel, parts=parts, pieces=len(moved[0])),
        "own_pass",
        [(keep, vmem), (outer_out, vmem), (inner_out, vmem)] + [(m, vmem) for per in moved for m in per],
        [
            (out_shape, F32, hbm),
            ((model // parts, width), F32, vmem),
            ((1, model // parts), F32, vmem),
        ],
        [pltpu.VMEM(out_shape, F32), pltpu.SemaphoreType.DMA(())],
    )


def final_kernel(own_qkv, own_gain, mirror_qkv, mirror_gains, gain_hbm, qkv_hbm, gain_ref, qkv_ref, sems):
    rows, width = qkv_ref.shape
    half = rows // 2
    lanes = mirror_gains.shape[1]
    lines = mirror_gains[...].astype(F32)
    for i in range(gain_ref.shape[1] // lanes):
        at = slice(i * lanes, (i + 1) * lanes)
        gain_ref[:, at] = own_gain[:, at] + lines[i : i + 1, :]
    copies = [pltpu.make_async_copy(gain_ref, gain_hbm, sems.at[0])]
    copies[0].start()
    for i in range(2):
        at = slice(i * half, (i + 1) * half)
        qkv_ref[at, :] = own_qkv[at, :] + mirror_qkv[at, :].astype(F32)
        copies.append(pltpu.make_async_copy(qkv_ref.at[at], qkv_hbm.at[at], sems.at[1 + i]))
        copies[-1].start()
    for copy in copies:
        copy.wait()


def final_pass(own_qkv, own_gain, mirror_qkv, mirror_gains):
    hbm, vmem = pltpu.HBM, pltpu.VMEM
    return call(
        final_kernel,
        "final_pass",
        [(own_qkv, vmem), (own_gain, vmem), (mirror_qkv, vmem), (mirror_gains, vmem)],
        [(own_gain.shape, F32, hbm), (own_qkv.shape, F32, hbm)],
        [pltpu.VMEM(own_gain.shape, F32), pltpu.VMEM(own_qkv.shape, F32), pltpu.SemaphoreType.DMA((3,))],
    )


def summed(keep, moved, at, rows):
    total = keep[at : at + rows, :].astype(F32)
    first, taken = 0, []
    for part in moved:
        low, high = max(at, first), min(at + rows, first + part.shape[1])
        if low < high:
            piece = part[0, low - first : high - first, :].astype(F32)
            for k in range(1, part.shape[0]):
                piece = piece + part[k, low - first : high - first, :].astype(F32)
            taken.append(piece)
        first += part.shape[1]
    return total + (taken[0] if len(taken) == 1 else jnp.concatenate(taken, axis=0))


def sum_kernel(keep, *refs, gains):
    moved, outs = refs[: -1 - bool(gains)], refs[-1 - bool(gains) :]
    rows = outs[0].shape[0]
    outs[0][...] = summed(keep, moved, 0, rows).astype(BF16)
    if gains:
        line = summed(keep, moved, rows, PAD)[:1, :gains]
        lanes = outs[1].shape[1]
        row = lax.broadcasted_iota(jnp.int32, outs[1].shape, 0)
        block = jnp.zeros(outs[1].shape, F32)
        for i in range(gains // lanes):
            block = jnp.where(row == i, line[:, i * lanes : (i + 1) * lanes], block)
        outs[1][...] = block.astype(BF16)


def sum_pass(keep, moved, gains=0, after=()):
    vmem = pltpu.VMEM
    pieces = [jnp.stack([per[p] for per in moved]) if len(moved) > 1 else moved[0][p][None] for p in range(len(moved[0]))]
    outputs = [((keep.shape[0] - (PAD if gains else 0), keep.shape[1]), BF16, vmem)]
    if gains:
        outputs += [((16 * pl.cdiv(gains, 16 * LANES), LANES), BF16, vmem)]
    return call(
        functools.partial(sum_kernel, gains=gains),
        "sum_pass", [(keep, vmem)] + [(p, vmem) for p in pieces], outputs, [], after,
    )


def shifted(value, axis, steps):
    count = lax.axis_size(axis)
    first, last = (max(0, -steps), min(count, count - steps))
    return lax.ppermute(value, axis, [(source, source + steps) for source in range(first, last)])


def mirrored(value, axis, sections=None):
    count = lax.axis_size(axis)
    return lax.ppermute(value, axis, [(i, count - 1 - i) for i in (range(count) if sections is None else sections)])


def exchanged(sends, axis):
    parts = lax.axis_size(axis)
    return [
        [lax.ppermute(send[k], axis, [(i, (i + 1 + k) % parts) for i in range(parts)]) for send in sends]
        for k in range(parts - 1)
    ]


def shards(
    act_down, act_up, grad_down, grad_up, seed_down, seed_up, gain_down, qkv_down, outproj_down,
    gain_up, qkv_up, outproj_up, doc_offsets, slot_order,
):
    parts = lax.axis_size("dp")
    query_width, model = outproj_down.shape[1:]
    width = qkv_down.shape[2]
    ints = (slot_order, doc_offsets.reshape(slot_order.shape))
    down = (gain_down, qkv_down[0], outproj_down[0])
    up = (gain_up, qkv_up[0], outproj_up[0])

    sections = lax.axis_size("section")
    edge = sections // 4
    outer = [*range(edge), *range(sections - edge, sections)]
    inner = range(edge, sections - edge)

    up_one = first_pass(1, ints, act_up[0], *up, grad_up[0], limit=FIRST_LIMIT)
    up_moved = shifted(up_one[0], "section", 1)
    down_one = first_pass(0, ints, act_down[0], *down, grad_down[0], limit=60 * 1024 * 1024, after=(up_one[4],))
    down_moved = shifted(down_one[0], "section", -1)
    up_forward = forward_pass(1, ints, act_up[0], gain_up, qkv_up[0], query_width)
    sends, keep = outproj_pass(1, up_one[2], up_forward[2], grad_up[0], up_moved, seed_up, parts)
    (up_out,) = sum_pass(keep, exchanged(sends, "dp"))
    outer_out = mirrored(up_out, "section", outer)
    inner_out = mirrored(up_out, "section", inner)
    up_two = backward_pass(
        1, slot_order, act_up[0], *up, seed_up, up_forward, up_one[4], up_moved, up_one[0], after=(up_out,)
    )
    sends, keep = qkv_pass(up_one[1], up_one[3], up_forward[0], up_two[1], up_two[2], parts, after=(down_moved,))
    down_forward = forward_pass(0, ints, act_down[0], gain_down, qkv_down[0], query_width, after=(keep,))
    up_qkv, up_gains = sum_pass(
        keep, exchanged(sends, "dp"), model // parts, after=(outer_out, down_forward[2])
    )
    mirror_gains = mirrored(up_gains, "section")
    mirror_qkv = mirrored(up_qkv, "section")
    down_two = backward_pass(
        0, slot_order, act_down[0], *down, seed_down, down_forward, down_one[4], down_moved, down_one[0],
        grads=up_two[3], after=(up_qkv, inner_out),
    )
    sends, keep = packed_pass(
        down_one[1], down_one[3], down_one[2], grad_down[0],
        down_forward[0], down_two[1], down_forward[2], down_two[0], down_two[2], parts,
    )
    grad_outproj, own_qkv, own_gain = own_pass(
        keep, outer_out, inner_out, exchanged(sends, "dp"), parts, query_width, model, width
    )
    grad_gain, grad_qkv = final_pass(own_qkv, own_gain, mirror_qkv, mirror_gains)
    return (down_two[3][:, None], grad_gain, grad_qkv[None], grad_outproj[None])


def solution(mesh):
    return jax.shard_map(
        shards,
        mesh=mesh,
        in_specs=(
            P("section", None, "dp", None),
            P("section", None, "dp", None),
            P("section", "dp", None),
            P("section", "dp", None),
            P("dp", None),
            P("dp", None),
            P("section", None),
            P("section", None, None),
            P("section", None, None),
            P("section", None),
            P("section", None, None),
            P("section", None, None),
            P(None, "section", None, "dp"),
            P(None, "section", None),
        ),
        out_specs=(
            P(None, "section", None, "dp", None),
            P("section", "dp"),
            P("section", "dp", None),
            P("section", "dp", None),
        ),
        check_vma=False,
    )
```

```python
import functools
import math
import jax
import jax.numpy as jnp
from jax import lax
from jax.experimental import pallas as pl
from jax.experimental.pallas import tpu as pltpu
from jax.sharding import PartitionSpec as P

HEADS = 8
KV_HEADS = 2
EPSILON = 1e-05
MASKED = -1e30
PAD = 16
LANES = 128
PACKED_PAD = 32
PIECES = 2
PIECES_OUT = 2
PIECES_QKV = 3
VMEM_LIMIT = 24 * 1024 * 1024
FIRST_LIMIT = 60 * 1024 * 1024
F32 = jnp.float32
BF16 = jnp.bfloat16
NN = (((1,), (0,)), ((), ()))
NT = (((1,), (1,)), ((), ()))
TN = (((0,), (0,)), ((), ()))


def dot(a, b, dims=NN):
    return lax.dot_general(a, b, dims, preferred_element_type=F32)


def doubled(pair, half):
    wide = pair.astype(F32)
    turned = pltpu.roll(wide, half, 1)
    left = lax.broadcasted_iota(jnp.int32, wide.shape, 1) < half
    zero = jnp.zeros_like(wide)
    out = []
    for g in range(KV_HEADS):
        a, b = (wide, turned) if g == 0 else (turned, wide)
        out.append(
            jnp.concatenate([jnp.where(left, a, zero), jnp.where(left, zero, b)], axis=0).astype(BF16)
        )
    return out


def mask_bias(seq, offset):
    row = lax.broadcasted_iota(jnp.int32, (seq, seq), 0)
    col = lax.broadcasted_iota(jnp.int32, (seq, seq), 1)
    start = jnp.where(row >= offset, offset, 0)
    return jnp.where((col <= row) & (col >= start), 0.0, MASKED).astype(F32)


def normalise(x, gain):
    xf = x.astype(F32)
    inverse = lax.rsqrt(jnp.mean(xf * xf, axis=1, keepdims=True) + EPSILON)
    scaled = xf * inverse
    return inverse, scaled, (scaled * gain).astype(BF16)


def softmax(scores):
    e = jnp.exp(scores - jnp.max(scores, axis=1, keepdims=True))
    return (e * (1.0 / jnp.sum(e, axis=1, keepdims=True))).astype(BF16)


def pair_columns(array, query_width):
    wide = 2 * (query_width // HEADS)
    return [array[:, p * wide : (p + 1) * wide] for p in range(HEADS // 2)]


def forward_heads(project, offset, query_width, soft_ref):
    seq = project.shape[0]
    half = query_width // HEADS
    wide = 2 * half
    keys = doubled(project[:, query_width : query_width + wide], half)
    values = doubled(project[:, query_width + wide :], half)
    bias = mask_bias(seq, offset)
    scale = jnp.asarray(half ** (-0.5), BF16)
    pairs = HEADS // 2
    group = [p * KV_HEADS // pairs for p in range(pairs)]
    queries = pair_columns(project, query_width)
    scores = [dot(queries[p] * scale, keys[group[p]], NT) for p in range(pairs)]
    for p in range(pairs):
        for t in range(2):
            at = slice(t * seq, (t + 1) * seq)
            soft_ref[p, :, at] = softmax(scores[p][:, at] + bias)
    return [dot(soft_ref[p], values[group[p]]) for p in range(pairs)]


def backward_heads(project, attended, grad_attended, query_width, soft_ref):
    seq = project.shape[0]
    half = query_width // HEADS
    wide = 2 * half
    keys = doubled(project[:, query_width : query_width + wide], half)
    values = doubled(project[:, query_width + wide :], half)
    scale = half ** (-0.5)
    pairs = HEADS // 2
    group = [p * KV_HEADS // pairs for p in range(pairs)]
    left = lax.broadcasted_iota(jnp.int32, (seq, wide), 1) < half
    queries = [q * jnp.asarray(scale, BF16) for q in pair_columns(project, query_width)]
    grads = pair_columns(grad_attended, query_width)
    grad_soft = [dot(grads[p], values[group[p]], NT) for p in range(pairs)]
    values_parts = [dot(grads[p], soft_ref[p], TN) for p in range(pairs)]
    grad_scores = []
    for p in range(pairs):
        both = attended[p].astype(F32) * grads[p].astype(F32)
        rows = [
            jnp.sum(jnp.where(left, both, 0.0), axis=1, keepdims=True),
            jnp.sum(jnp.where(left, 0.0, both), axis=1, keepdims=True),
        ]
        columns = [slice(t * seq, (t + 1) * seq) for t in range(2)]
        grad_scores.append(
            jnp.concatenate(
                [
                    (soft_ref[p, :, at].astype(F32) * (grad_soft[p][:, at] - row)).astype(BF16)
                    for at, row in zip(columns, rows)
                ],
                axis=1,
            )
        )
    grad_queries = [dot(grad_scores[p], keys[group[p]]) * scale for p in range(pairs)]
    keys_parts = [dot(queries[p], grad_scores[p], TN) for p in range(pairs)]

    def joined(parts):
        sums = []
        for g in range(KV_HEADS):
            part = sum(parts[p] for p in range(pairs) if group[p] == g)
            sums.append(part[:half, :seq] + part[half:, seq:])
        return jnp.concatenate(sums, axis=0).T

    columns = [*grad_queries, joined(keys_parts), joined(values_parts)]
    return jnp.concatenate([c.astype(BF16) for c in columns], axis=1)


def input_gradient(grad_project, qkv, gain, scaled, inverse, upstream):
    grad_normed = dot(grad_project, qkv, NT)
    grad_hat = grad_normed * gain
    part = grad_normed * scaled
    grad_gain = jnp.sum(part, axis=0, keepdims=True)
    mean = jnp.mean(part * gain, axis=1, keepdims=True)
    grad_in = upstream.astype(F32) + inverse * (grad_hat - scaled * mean)
    return grad_in.astype(BF16), grad_gain


def whole(memory=pltpu.VMEM):
    return pl.BlockSpec(memory_space=memory)


def call(kernel, name, inputs, outputs, scratch, after=(), aliases=None, limit=VMEM_LIMIT):
    count = len(inputs)

    def ordered(*refs):
        kernel(*refs[:count], *refs[count + len(after) :])

    return pl.pallas_call(
        ordered,
        out_shape=tuple(jax.ShapeDtypeStruct(shape, dtype) for shape, dtype, _ in outputs),
        in_specs=[whole(space) for _, space in inputs] + [whole(pl.ANY)] * len(after),
        out_specs=tuple(whole(space) for _, _, space in outputs),
        scratch_shapes=scratch,
        input_output_aliases=aliases or {},
        compiler_params=pltpu.CompilerParams(vmem_limit_bytes=limit),
        cost_estimate=pl.CostEstimate(flops=1, bytes_accessed=1, transcendentals=0),
        name=name,
    )(*(array for array, _ in inputs), *after)


def start_all(sources, targets, sems):
    copies = [pltpu.make_async_copy(a, b, sems.at[i]) for i, (a, b) in enumerate(zip(sources, targets))]
    for copy in copies:
        copy.start()
    return copies


def first_kernel(order, offsets, act, qkv_hbm, out_hbm, up_hbm, gain_hbm, *refs, direction):
    grad_ref, normed_ref, attended_ref, project_ref, gain_out = refs[:5]
    order_ref, offsets_ref, x_ref, qkv_ref, out_ref, up_ref, gain_ref, soft_ref, sems = refs[5:]
    sources = (order, offsets, gain_hbm, act, qkv_hbm, up_hbm, out_hbm)
    targets = (order_ref, offsets_ref, gain_ref, x_ref, qkv_ref, up_ref, out_ref)
    copies = [pltpu.make_async_copy(a, b, sems.at[i]) for i, (a, b) in enumerate(zip(sources, targets))]
    for copy in copies[:5]:
        copy.start()
    query_width = out_hbm.shape[0]
    for copy in copies[:4]:
        copy.wait()
    for copy in copies[5:]:
        copy.start()
    which = order_ref[direction, 0, 0]
    offset = offsets_ref[direction, 0, which]
    gain = gain_ref[...]
    _, _, normed = normalise(x_ref[which], gain)
    normed_ref[...] = normed
    copies[4].wait()
    project = dot(normed, qkv_ref[...]).astype(BF16)
    attended = forward_heads(project, offset, query_width, soft_ref)
    attended_ref[...] = jnp.concatenate([a.astype(BF16) for a in attended], axis=1)
    copies[5].wait()
    copies[6].wait()
    grad_attended = dot(up_ref[...], out_ref[...], NT).astype(BF16)
    grad_project = backward_heads(project, attended, grad_attended, query_width, soft_ref)
    project_ref[...] = grad_project
    inverse, scaled, _ = normalise(x_ref[which], gain)
    grad_ref[...], gain_out[...] = input_gradient(grad_project, qkv_ref[...], gain, scaled, inverse, up_ref[...])


def first_pass(direction, ints, act, gain, qkv, out, upstream, after=(), limit=VMEM_LIMIT):
    seq, model = act.shape[1:]
    width = qkv.shape[1]
    query_width = out.shape[0]
    hbm, vmem = pltpu.HBM, pltpu.VMEM
    return call(
        functools.partial(first_kernel, direction=direction),
        "first_pass",
        [(a, hbm) for a in (*ints, act, qkv, out, upstream, gain)],
        [
            ((seq, model), BF16, vmem),
            ((seq, model), BF16, vmem),
            ((seq, query_width), BF16, vmem),
            ((seq, width), BF16, vmem),
            ((1, model), F32, vmem),
        ],
        [pltpu.SMEM(a.shape, jnp.int32) for a in ints]
        + [
            pltpu.VMEM(act.shape, BF16),
            pltpu.VMEM((model, width), BF16),
            pltpu.VMEM((query_width, model), BF16),
            pltpu.VMEM((seq, model), BF16),
            pltpu.VMEM((1, model), F32),
            pltpu.VMEM((HEADS // 2, seq, 2 * seq), BF16),
            pltpu.SemaphoreType.DMA((7,)),
        ],
        after,
        limit=limit,
    )


def forward_kernel(order, offsets, act, qkv_hbm, gain_hbm, *refs, direction, query_width):
    normed_ref, project_ref, attended_ref, soft_ref = refs[:4]
    order_ref, offsets_ref, x_ref, qkv_ref, gain_ref, sems = refs[4:]
    copies = start_all(
        (order, offsets, act, gain_hbm, qkv_hbm), (order_ref, offsets_ref, x_ref, gain_ref, qkv_ref), sems
    )
    for copy in copies[:4]:
        copy.wait()
    which = order_ref[direction, 0, 1]
    offset = offsets_ref[direction, 0, which]
    _, _, normed = normalise(x_ref[which], gain_ref[...])
    normed_ref[...] = normed
    copies[4].wait()
    project = dot(normed, qkv_ref[...]).astype(BF16)
    project_ref[...] = project
    attended = forward_heads(project, offset, query_width, soft_ref)
    attended_ref[...] = jnp.concatenate([a.astype(BF16) for a in attended], axis=1)


def forward_pass(direction, ints, act, gain, qkv, query_width, after=()):
    seq, model = act.shape[1:]
    width = qkv.shape[1]
    hbm, vmem = pltpu.HBM, pltpu.VMEM
    return call(
        functools.partial(forward_kernel, direction=direction, query_width=query_width),
        "forward_pass",
        [(a, hbm) for a in (*ints, act, qkv, gain)],
        [
            ((seq, model), BF16, vmem),
            ((seq, width), BF16, vmem),
            ((seq, query_width), BF16, vmem),
            ((HEADS // 2, seq, 2 * seq), BF16, vmem),
        ],
        [pltpu.SMEM(a.shape, jnp.int32) for a in ints]
        + [
            pltpu.VMEM(act.shape, BF16),
            pltpu.VMEM((model, width), BF16),
            pltpu.VMEM((1, model), F32),
            pltpu.SemaphoreType.DMA((5,)),
        ],
        after,
    )


def choose_upstream(direction, moved, seed_hbm, up_ref, sem):
    seeded = lax.axis_index("section") == (lax.axis_size("section") - 1 if direction == 0 else 0)

    @pl.when(seeded)
    def _():
        copy = pltpu.make_async_copy(seed_hbm, up_ref, sem)
        copy.start()
        copy.wait()

    @pl.when(jnp.logical_not(seeded))
    def _():
        up_ref[...] = moved[...]


def backward_kernel(
    order, act, qkv_hbm, out_hbm, gain_hbm, seed_hbm, project_ref, attended_ref, soft_ref, gain1, moved, own,
    *refs, direction, kept,
):
    up_ref, gproj_ref, gain_out, grads_hbm = refs[kept : kept + 4]
    order_ref, x_ref, qkv_ref, out_ref, gain_ref, grad_ref, sems = refs[kept + 4 :]
    copies = start_all(
        (order, act, gain_hbm, out_hbm, qkv_hbm), (order_ref, x_ref, gain_ref, out_ref, qkv_ref), sems
    )
    choose_upstream(direction, moved, seed_hbm, up_ref, sems.at[5])
    copies[3].wait()
    query_width = out_ref.shape[0]
    wide = 2 * query_width // HEADS
    grad_attended = dot(up_ref[...], out_ref[...], NT).astype(BF16)
    attended = [attended_ref[:, p * wide : (p + 1) * wide] for p in range(HEADS // 2)]
    gproj_ref[...] = backward_heads(project_ref[...], attended, grad_attended, query_width, soft_ref)
    for at in (0, 1, 2, 4):
        copies[at].wait()
    gain = gain_ref[...]
    inverse, scaled, _ = normalise(x_ref[order_ref[direction, 0, 1]], gain)
    grad_ref[0] = own[...]
    grad_ref[1], grad_gain = input_gradient(gproj_ref[...], qkv_ref[...], gain, scaled, inverse, up_ref[...])
    gain_out[...] = gain1[...] + grad_gain
    written = pltpu.make_async_copy(grad_ref, grads_hbm.at[direction], sems.at[6])
    written.start()
    written.wait()


def backward_pass(direction, order, act, gain, qkv, out, seed, forward, gain1, moved, own, grads=None, after=()):
    seq, model = act.shape[1:]
    width = qkv.shape[1]
    query_width = out.shape[0]
    hbm, vmem = pltpu.HBM, pltpu.VMEM
    _, project, attended, soft = forward
    inputs = [(a, hbm) for a in (order, act, qkv, out, gain, seed)]
    inputs += [(a, vmem) for a in (project, attended, soft, gain1, moved, own)]
    aliases = {}
    if grads is not None:
        aliases = {len(inputs): 3}
        inputs += [(grads, hbm)]
    return call(
        functools.partial(backward_kernel, direction=direction, kept=len(aliases)),
        "backward_pass",
        inputs,
        [
            ((seq, model), BF16, vmem),
            ((seq, width), BF16, vmem),
            ((1, model), F32, vmem),
            ((2, 2, seq, model), BF16, hbm),
        ],
        [
            pltpu.SMEM(order.shape, jnp.int32),
            pltpu.VMEM(act.shape, BF16),
            pltpu.VMEM((model, width), BF16),
            pltpu.VMEM((query_width, model), BF16),
            pltpu.VMEM((1, model), F32),
            pltpu.VMEM((2, seq, model), BF16),
            pltpu.SemaphoreType.DMA((7,)),
        ],
        after,
        aliases,
    )


def cut(rows, pieces):
    return max(p for p in range(1, pieces + 1) if rows % (16 * p) == 0)


def hand_out(blocks, sends, keep_ref):
    parts = blocks.shape[0]
    replica = lax.axis_index("dp")
    for k in range(parts - 1):
        at = lax.rem(replica + 1 + k, parts)
        for p, ref in enumerate(sends):
            rows = ref.shape[1]
            ref[k] = blocks[at, p * rows : (p + 1) * rows, :]
    keep_ref[...] = blocks[replica]


def outproj_kernel(up_hbm, seed_hbm, att1, att2, moved, *refs, direction):
    *sends, keep_ref, up1_ref, up2_ref, blocks, sems = refs
    copy = pltpu.make_async_copy(up_hbm, up1_ref, sems.at[0])
    copy.start()
    choose_upstream(direction, moved, seed_hbm, up2_ref, sems.at[1])
    parts, rows, _ = blocks.shape
    copy.wait()
    total = dot(att1[...], up1_ref[...], TN) + dot(att2[...], up2_ref[...], TN)
    for q in range(parts):
        blocks[q] = total[q * rows : (q + 1) * rows].astype(BF16)
    hand_out(blocks, sends, keep_ref)


def outproj_pass(direction, att1, att2, upstream, moved, seed, parts, after=()):
    seq, model = moved.shape
    rows = att1.shape[1] // parts
    pieces = cut(rows, PIECES_OUT)
    hbm, vmem = pltpu.HBM, pltpu.VMEM
    *sends, keep = call(
        functools.partial(outproj_kernel, direction=direction),
        "outproj_pass",
        [(upstream, hbm), (seed, hbm), (att1, vmem), (att2, vmem), (moved, vmem)],
        [((parts - 1, rows // pieces, model), BF16, vmem)] * pieces + [((rows, model), BF16, vmem)],
        [
            pltpu.VMEM((seq, model), BF16),
            pltpu.VMEM((seq, model), BF16),
            pltpu.VMEM((parts, rows, model), BF16),
            pltpu.SemaphoreType.DMA((2,)),
        ],
        after,
    )
    return sends, keep


def qkv_kernel(normed1, gproj1, normed2, gproj2, gain, *refs):
    *sends, keep_ref, blocks = refs
    parts, height, width = blocks.shape
    rows = normed1.shape[1] // parts
    for q in range(parts):
        at = slice(q * rows, (q + 1) * rows)
        total = dot(normed1[:, at], gproj1[...], TN) + dot(normed2[:, at], gproj2[...], TN)
        blocks[q, :rows, :] = total.astype(BF16)
        blocks[q, rows:, :] = jnp.zeros((height - rows, width), BF16)
        blocks[q, rows:, :rows] = jnp.broadcast_to(gain[:, at], (height - rows, rows)).astype(BF16)
    hand_out(blocks, sends, keep_ref)


def qkv_pass(normed1, gproj1, normed2, gproj2, gain, parts, after=()):
    rows, width = normed1.shape[1] // parts + PAD, gproj1.shape[1]
    pieces = cut(rows, PIECES_QKV)
    vmem = pltpu.VMEM
    *sends, keep = call(
        qkv_kernel,
        "qkv_pass",
        [(a, vmem) for a in (normed1, gproj1, normed2, gproj2, gain)],
        [((parts - 1, rows // pieces, width), BF16, vmem)] * pieces + [((rows, width), BF16, vmem)],
        [pltpu.VMEM((parts, rows, width), BF16)],
        after,
    )
    return sends, keep


def layout(parts, query_width, model, width):
    unit = math.gcd(model, width)
    out_rows, qkv_rows = query_width // parts, model // parts
    start = out_rows * (model // unit)
    gain_at = start + qkv_rows * (width // unit)
    return unit, out_rows, qkv_rows, start, gain_at, gain_at + PACKED_PAD


def packed_kernel(normed1, gproj1, att1, up1_hbm, normed2, gproj2, att2, up2, gain, *refs):
    *sends, keep_ref, blocks, up1, sem = refs
    copy = pltpu.make_async_copy(up1_hbm, up1, sem)
    copy.start()
    parts = blocks.shape[0]
    model, width = normed1.shape[1], gproj1.shape[1]
    unit, out_rows, qkv_rows, start, gain_at, _ = layout(parts, att1.shape[1], model, width)
    row = lax.broadcasted_iota(jnp.int32, (PACKED_PAD, unit), 0)
    for q in range(parts):
        at = slice(q * qkv_rows, (q + 1) * qkv_rows)
        qkv = dot(normed1[:, at], gproj1[...], TN) + dot(normed2[:, at], gproj2[...], TN)
        for c in range(width // unit):
            first = start + c * qkv_rows
            blocks[q, first : first + qkv_rows, :] = qkv[:, c * unit : (c + 1) * unit].astype(BF16)
        lines = jnp.zeros((PACKED_PAD, unit), F32)
        for i in range(pl.cdiv(qkv_rows, unit)):
            line = gain[:, q * qkv_rows + i * unit : q * qkv_rows + min((i + 1) * unit, qkv_rows)]
            if line.shape[1] < unit:
                line = jnp.concatenate([line, jnp.zeros((1, unit - line.shape[1]), F32)], axis=1)
            lines = jnp.where(row == i, line, lines)
        blocks[q, gain_at:, :] = lines.astype(BF16)
    copy.wait()
    out = dot(att1[...], up1[...], TN) + dot(att2[...], up2[...], TN)
    for q in range(parts):
        for c in range(model // unit):
            blocks[q, c * out_rows : (c + 1) * out_rows, :] = out[
                q * out_rows : (q + 1) * out_rows, c * unit : (c + 1) * unit
            ].astype(BF16)
    hand_out(blocks, sends, keep_ref)


def packed_pass(normed1, gproj1, att1, up1, normed2, gproj2, att2, up2, gain, parts, after=()):
    seq, model = normed1.shape
    unit, _, _, _, _, rows = layout(parts, att1.shape[1], model, gproj1.shape[1])
    pieces = cut(rows, PIECES)
    hbm, vmem = pltpu.HBM, pltpu.VMEM
    *sends, keep = call(
        packed_kernel,
        "packed_pass",
        [(normed1, vmem), (gproj1, vmem), (att1, vmem), (up1, hbm)]
        + [(a, vmem) for a in (normed2, gproj2, att2, up2, gain)],
        [((parts - 1, rows // pieces, unit), BF16, vmem)] * pieces + [((rows, unit), BF16, vmem)],
        [
            pltpu.VMEM((parts, rows, unit), BF16),
            pltpu.VMEM((seq, model), BF16),
            pltpu.SemaphoreType.DMA(()),
        ],
        after,
    )
    return sends, keep


def own_kernel(keep, outer_out, inner_out, *refs, parts, pieces):
    moved, refs = refs[: (parts - 1) * pieces], refs[(parts - 1) * pieces :]
    out_hbm, qkv_ref, gain_ref, out_ref, sem = refs
    model, width = out_ref.shape[1], qkv_ref.shape[1]
    unit, out_rows, qkv_rows, start, gain_at, rows = layout(parts, out_ref.shape[0] * parts, model, width)
    each = rows // pieces

    def total(first, count):
        result = keep[first : first + count, :].astype(F32)
        for k in range(parts - 1):
            taken, at = [], first
            while at < first + count:
                p = at // each
                until = min(first + count, (p + 1) * each)
                taken.append(moved[k * pieces + p][at - p * each : until - p * each, :].astype(F32))
                at = until
            result = result + (taken[0] if len(taken) == 1 else jnp.concatenate(taken, axis=0))
        return result

    for c in range(model // unit):
        columns = slice(c * unit, (c + 1) * unit)
        out_ref[:, columns] = total(c * out_rows, out_rows) + (outer_out[:, columns] + inner_out[:, columns]).astype(F32)
    copy = pltpu.make_async_copy(out_ref, out_hbm, sem)
    copy.start()
    for c in range(width // unit):
        qkv_ref[:, c * unit : (c + 1) * unit] = total(start + c * qkv_rows, qkv_rows)
    lines = total(gain_at, PACKED_PAD)
    for i in range(pl.cdiv(qkv_rows, unit)):
        until = min((i + 1) * unit, qkv_rows)
        gain_ref[:, i * unit : until] = lines[i : i + 1, : until - i * unit]
    copy.wait()


def own_pass(keep, outer_out, inner_out, moved, parts, query_width, model, width):
    hbm, vmem = pltpu.HBM, pltpu.VMEM
    out_shape = (query_width // parts, model)
    return call(
        functools.partial(own_kernel, parts=parts, pieces=len(moved[0])),
        "own_pass",
        [(keep, vmem), (outer_out, vmem), (inner_out, vmem)] + [(m, vmem) for per in moved for m in per],
        [
            (out_shape, F32, hbm),
            ((model // parts, width), F32, vmem),
            ((1, model // parts), F32, vmem),
        ],
        [pltpu.VMEM(out_shape, F32), pltpu.SemaphoreType.DMA(())],
    )


def final_kernel(own_qkv, own_gain, mirror_qkv, mirror_gains, gain_hbm, qkv_hbm, gain_ref, qkv_ref, sems):
    rows, width = qkv_ref.shape
    half = rows // 2
    lanes = mirror_gains.shape[1]
    lines = mirror_gains[...].astype(F32)
    for i in range(gain_ref.shape[1] // lanes):
        at = slice(i * lanes, (i + 1) * lanes)
        gain_ref[:, at] = own_gain[:, at] + lines[i : i + 1, :]
    copies = [pltpu.make_async_copy(gain_ref, gain_hbm, sems.at[0])]
    copies[0].start()
    for i in range(2):
        at = slice(i * half, (i + 1) * half)
        qkv_ref[at, :] = own_qkv[at, :] + mirror_qkv[at, :].astype(F32)
        copies.append(pltpu.make_async_copy(qkv_ref.at[at], qkv_hbm.at[at], sems.at[1 + i]))
        copies[-1].start()
    for copy in copies:
        copy.wait()


def final_pass(own_qkv, own_gain, mirror_qkv, mirror_gains):
    hbm, vmem = pltpu.HBM, pltpu.VMEM
    return call(
        final_kernel,
        "final_pass",
        [(own_qkv, vmem), (own_gain, vmem), (mirror_qkv, vmem), (mirror_gains, vmem)],
        [(own_gain.shape, F32, hbm), (own_qkv.shape, F32, hbm)],
        [pltpu.VMEM(own_gain.shape, F32), pltpu.VMEM(own_qkv.shape, F32), pltpu.SemaphoreType.DMA((3,))],
    )


def summed(keep, moved, at, rows):
    total = keep[at : at + rows, :].astype(F32)
    first, taken = 0, []
    for part in moved:
        low, high = max(at, first), min(at + rows, first + part.shape[1])
        if low < high:
            piece = part[0, low - first : high - first, :].astype(F32)
            for k in range(1, part.shape[0]):
                piece = piece + part[k, low - first : high - first, :].astype(F32)
            taken.append(piece)
        first += part.shape[1]
    return total + (taken[0] if len(taken) == 1 else jnp.concatenate(taken, axis=0))


def sum_kernel(keep, *refs, gains):
    moved, outs = refs[: -1 - bool(gains)], refs[-1 - bool(gains) :]
    rows = outs[0].shape[0]
    outs[0][...] = summed(keep, moved, 0, rows).astype(BF16)
    if gains:
        line = summed(keep, moved, rows, PAD)[:1, :gains]
        lanes = outs[1].shape[1]
        row = lax.broadcasted_iota(jnp.int32, outs[1].shape, 0)
        block = jnp.zeros(outs[1].shape, F32)
        for i in range(gains // lanes):
            block = jnp.where(row == i, line[:, i * lanes : (i + 1) * lanes], block)
        outs[1][...] = block.astype(BF16)


def sum_pass(keep, moved, gains=0, after=()):
    vmem = pltpu.VMEM
    pieces = [jnp.stack([per[p] for per in moved]) if len(moved) > 1 else moved[0][p][None] for p in range(len(moved[0]))]
    outputs = [((keep.shape[0] - (PAD if gains else 0), keep.shape[1]), BF16, vmem)]
    if gains:
        outputs += [((16 * pl.cdiv(gains, 16 * LANES), LANES), BF16, vmem)]
    return call(
        functools.partial(sum_kernel, gains=gains),
        "sum_pass", [(keep, vmem)] + [(p, vmem) for p in pieces], outputs, [], after,
    )


def shifted(value, axis, steps):
    count = lax.axis_size(axis)
    first, last = (max(0, -steps), min(count, count - steps))
    return lax.ppermute(value, axis, [(source, source + steps) for source in range(first, last)])


def mirrored(value, axis, sections=None):
    count = lax.axis_size(axis)
    return lax.ppermute(value, axis, [(i, count - 1 - i) for i in (range(count) if sections is None else sections)])


def exchanged(sends, axis):
    parts = lax.axis_size(axis)
    return [
        [lax.ppermute(send[k], axis, [(i, (i + 1 + k) % parts) for i in range(parts)]) for send in sends]
        for k in range(parts - 1)
    ]


def shards(
    act_down, act_up, grad_down, grad_up, seed_down, seed_up, gain_down, qkv_down, outproj_down,
    gain_up, qkv_up, outproj_up, doc_offsets, slot_order,
):
    parts = lax.axis_size("dp")
    query_width, model = outproj_down.shape[1:]
    width = qkv_down.shape[2]
    ints = (slot_order, doc_offsets.reshape(slot_order.shape))
    down = (gain_down, qkv_down[0], outproj_down[0])
    up = (gain_up, qkv_up[0], outproj_up[0])

    sections = lax.axis_size("section")
    edge = sections // 4
    outer = [*range(edge), *range(sections - edge, sections)]
    inner = range(edge, sections - edge)

    up_one = first_pass(1, ints, act_up[0], *up, grad_up[0], limit=FIRST_LIMIT)
    up_moved = shifted(up_one[0], "section", 1)
    down_one = first_pass(0, ints, act_down[0], *down, grad_down[0], limit=60 * 1024 * 1024, after=(up_one[4],))
    down_moved = shifted(down_one[0], "section", -1)
    up_forward = forward_pass(1, ints, act_up[0], gain_up, qkv_up[0], query_width)
    sends, keep = outproj_pass(1, up_one[2], up_forward[2], grad_up[0], up_moved, seed_up, parts)
    (up_out,) = sum_pass(keep, exchanged(sends, "dp"))
    outer_out = mirrored(up_out, "section", range(edge))
    inner_out = mirrored(up_out, "section", range(edge, sections))
    up_two = backward_pass(
        1, slot_order, act_up[0], *up, seed_up, up_forward, up_one[4], up_moved, up_one[0], after=(up_out,)
    )
    sends, keep = qkv_pass(up_one[1], up_one[3], up_forward[0], up_two[1], up_two[2], parts, after=(down_moved,))
    down_forward = forward_pass(0, ints, act_down[0], gain_down, qkv_down[0], query_width, after=(keep,))
    up_qkv, up_gains = sum_pass(
        keep, exchanged(sends, "dp"), model // parts, after=(outer_out,)
    )
    mirror_gains = mirrored(up_gains, "section")
    mirror_qkv = mirrored(up_qkv, "section")
    down_two = backward_pass(
        0, slot_order, act_down[0], *down, seed_down, down_forward, down_one[4], down_moved, down_one[0],
        grads=up_two[3], after=(up_qkv, inner_out),
    )
    sends, keep = packed_pass(
        down_one[1], down_one[3], down_one[2], grad_down[0],
        down_forward[0], down_two[1], down_forward[2], down_two[0], down_two[2], parts,
    )
    grad_outproj, own_qkv, own_gain = own_pass(
        keep, outer_out, inner_out, exchanged(sends, "dp"), parts, query_width, model, width
    )
    grad_gain, grad_qkv = final_pass(own_qkv, own_gain, mirror_qkv, mirror_gains)
    return (down_two[3][:, None], grad_gain, grad_qkv[None], grad_outproj[None])


def solution(mesh):
    return jax.shard_map(
        shards,
        mesh=mesh,
        in_specs=(
            P("section", None, "dp", None),
            P("section", None, "dp", None),
            P("section", "dp", None),
            P("section", "dp", None),
            P("dp", None),
            P("dp", None),
            P("section", None),
            P("section", None, None),
            P("section", None, None),
            P("section", None),
            P("section", None, None),
            P("section", None, None),
            P(None, "section", None, "dp"),
            P(None, "section", None),
        ),
        out_specs=(
            P(None, "section", None, "dp", None),
            P("section", "dp"),
            P("section", "dp", None),
            P("section", "dp", None),
        ),
        check_vma=False,
    )
```
